256 devices in a mesh: dp: 64 (over y_lo, z, x), tensor: 4 (over y_hi, core).
Axes of the slice: x: 4, y: 4 (y_hi: 2, y_lo: 2; y = y_hi * 2 + y_lo), z: 8, core: 2. Of those that a mesh axis runs over, the one named last changes fastest.
Arguments:
- features: bfloat16 [14336, 12288], P('dp', 'tensor'), may hold values from -6 to 6
- weights: bfloat16 [1536, 96, 128], P(None, 'tensor'), may hold values from -0.109375 to 0.109375
- block_cols: int32 [96, 12], P('tensor'), may hold values from 0 to 47, as said below
- cotangent: bfloat16 [14336, 6144], P('dp', 'tensor'), may hold values from -6 to 6
Outputs:
- input_grad: bfloat16 [14336, 12288], P('dp', 'tensor')
- weight_grad: float32 [1536, 96, 128], P('dp', 'tensor')
The draws below stay inside these ranges and needn't reach their ends.
Inputs may be any that keep to these rules, and one draw needn't show every extreme that they name: Each row of block_cols names 12 distinct block columns; in each aligned group of four block rows the four rows name disjoint sets, so every block column is named by exactly one row of each group.
All inputs are finite; a program needn't handle non-finite values.
Results may differ from the reference program's by a relative error of at most 0.0049.
Values may be sent and summed in bfloat16 or wider, within the bound.
A program may use at most 192 MiB of HBM per device.

```python
import jax
import jax.numpy as jnp
from jax import lax

D = 12288
DOUT = 6144
BS = 128
NBR = 96
NCB = 48
KB = 12
TOKENS = 14336


def choose_group(subkey):
    return jax.random.permutation(subkey, NCB)


def draw_block_cols(key, part):
    key = jax.random.fold_in(key, 7)
    group_keys = jax.random.split(key, NBR // 4)
    orders = jax.vmap(choose_group)(group_keys)
    return orders.reshape(NBR, KB).astype(jnp.int32)


def block_levels(rng, dims, shards, least, top_value):
    gain = 1.0
    for dim, shards_of in shards:
        draws = jax.random.uniform(jax.random.fold_in(jax.random.fold_in(rng, 6), dim), (shards_of,), jnp.float32, least / len(shards), top_value / len(shards))
        gain = gain * jnp.repeat(jnp.exp(draws), dims[dim] // shards_of).reshape((-1,) + (1,) * (len(dims) - 1 - dim))
    return gain


def normal_values(own_key, dims, deviation, bound, cuts=(), held_as=jnp.bfloat16):
    result = deviation * jax.random.normal(own_key, dims, jnp.float32)
    if cuts:
        result = result * block_levels(own_key, dims, cuts, -0.22, 0.18)
    return jnp.clip(result, -bound, bound).astype(held_as)


def setup_inputs(seed: int = 0) -> dict:
    key_list = jax.random.split(jax.random.key(seed), 5)
    return {
        "features": normal_values(key_list[0], (TOKENS, D), 1.0, 6.0, ((0, 64), (1, 4))),
        "weights": normal_values(key_list[1], (KB * BS, NBR, BS), (D // 4) ** -0.5, 0.109375, ((1, 4),)),
        "block_cols": draw_block_cols(jax.random.fold_in(key_list[4], 71), 0),
        "cotangent": normal_values(key_list[3], (TOKENS, DOUT), 1.0, 6.0, ((0, 64), (1, 4))),
    }


gelu_coef = 0.7978845608


def gelu_slope(pre_act):
    inner_arg = gelu_coef * (pre_act + 0.044715 * pre_act * pre_act * pre_act)
    tanh_val = jnp.tanh(inner_arg)
    return 0.5 * (1.0 + tanh_val) + 0.5 * pre_act * (1.0 - tanh_val * tanh_val) * gelu_coef * (1.0 + 0.134145 * pre_act * pre_act)


def reference(features, weights, block_cols, cotangent):
    blocks = weights.reshape(KB, BS, NBR, BS)
    columns = jnp.arange(NCB, dtype=jnp.int32)

    def forward_row(running, row_index):
        inputs = lax.dynamic_slice_in_dim(features, row_index * BS, BS, 1).astype(jnp.float32)
        chosen = lax.dynamic_index_in_dim(blocks, row_index, 2, keepdims=False).astype(jnp.float32)
        col_ids = lax.dynamic_index_in_dim(block_cols, row_index, 0, keepdims=False)
        onehot = (col_ids[:, None] == columns[None, :]).astype(jnp.float32)
        products = jnp.einsum("ti,kij->tkj", inputs, chosen)
        added = jnp.einsum("tkj,kc->tcj", products, onehot, precision=lax.Precision.HIGHEST)
        return running + added, None

    empty_sum = jnp.zeros((TOKENS, NCB, BS), jnp.float32)
    row_ids = jnp.arange(NBR, dtype=jnp.int32)
    full_sum, _ = lax.scan(forward_row, empty_sum, row_ids)
    upstream = cotangent.reshape(TOKENS, NCB, BS).astype(jnp.float32)
    slope = (upstream * gelu_slope(full_sum)).astype(jnp.bfloat16)
    grad_scale = TOKENS ** -0.5

    def backward_row(carry, row_index):
        inputs = lax.dynamic_slice_in_dim(features, row_index * BS, BS, 1).astype(jnp.float32)
        chosen = lax.dynamic_index_in_dim(blocks, row_index, 2, keepdims=False).astype(jnp.float32)
        col_ids = lax.dynamic_index_in_dim(block_cols, row_index, 0, keepdims=False)
        picked = jnp.take(slope, col_ids, axis=1).astype(jnp.float32)
        grad_rows = jnp.einsum("tkj,kij->ti", picked, chosen).astype(jnp.bfloat16)
        grad_blocks = jnp.einsum("ti,tkj->kij", inputs, picked) * grad_scale
        return carry, (grad_rows, grad_blocks)

    _, (grads_in, grads_w) = lax.scan(backward_row, None, row_ids)
    input_grad = jnp.transpose(grads_in, (1, 0, 2)).reshape(TOKENS, D)
    weight_grad = jnp.transpose(grads_w, (1, 2, 0, 3)).reshape(KB * BS, NBR, BS)
    return (input_grad, weight_grad)
```

```python
import functools

import jax
import jax.numpy as jnp
from jax import lax
from jax.experimental import pallas as pl
from jax.experimental.pallas import tpu as pltpu
from jax.sharding import PartitionSpec as P

MESH = pl.DeviceIdType.MESH
F32 = jnp.float32
BF16 = jnp.bfloat16
gelu_coef = 0.7978845608

ORDER = (
    [("W", 2, 0), ("xs", 0, 0), ("xs", 1, 0), ("W", 0, 0), ("zs", 0, 0), ("zs", 1, 0), ("W", 1, 0), ("W", 3, 0), ("D", 3, 0)]
    + [("zt", 0, 0), ("zt", 1, 0), ("zs", 2, 0), ("zs", 3, 0), ("xt", 0, 0), ("xt", 1, 0), ("xs", 2, 0), ("xs", 3, 0), ("D", 3, 0)]
    + [("zt", 0, 1), ("zt", 1, 1), ("D", 3, 0), ("zt", 2, 0), ("zt", 3, 0), ("xt", 0, 1), ("xt", 1, 1), ("us", 0, 0), ("us", 1, 0), ("D", 3, 0)]
    + [("zt", 0, 2), ("zt", 1, 2), ("D", 3, 0), ("ut", 0, 0), ("ut", 1, 0), ("zt", 2, 1), ("zt", 3, 1), ("xt", 2, 0), ("xt", 3, 0), ("D", 3, 0), ("ut", 0, 1), ("ut", 1, 1)]
    + [("zt", 0, 3), ("zt", 1, 3), ("vs", 0, 0), ("vs", 1, 0), ("zt", 2, 2), ("zt", 3, 2), ("D", 3, 0), ("ut", 0, 2), ("ut", 1, 2), ("vt", 0, 0), ("vt", 1, 0), ("xt", 2, 1), ("xt", 3, 1), ("us", 2, 0), ("us", 3, 0), ("D", 3, 0)]
    + [("ut", 0, 3), ("ut", 1, 3), ("ys", 2, 0), ("vt", 0, 1), ("vt", 1, 1), ("ys", 0, 0), ("ut", 2, 0), ("ut", 3, 0), ("zt", 2, 3), ("zt", 3, 3), ("vs", 2, 0), ("vs", 3, 0)]
    + [("ut", 2, 1), ("ut", 3, 1), ("vt", 2, 0), ("vt", 3, 0), ("ut", 2, 2), ("ut", 3, 2), ("vt", 2, 1), ("vt", 3, 1), ("ys", 1, 0), ("ut", 2, 3), ("ut", 3, 3), ("ys", 3, 0)]
    + [("yt", 2, 0), ("yt", 0, 0), ("yt", 1, 0), ("yt", 3, 0)]
)


def gelu_slope(v):
    th = jnp.tanh(gelu_coef * (v + 0.044715 * v * v * v))
    return 0.5 * (1.0 + th) + 0.5 * v * (1.0 - th * th) * gelu_coef * (1.0 + 0.134145 * v * v)


class Ring:
    def __init__(self, n, pos, ahead, back, load, own, send, recv, ssem, rsem):
        self.n, self.pos, self.devs, self.load, self.own = n, pos, (ahead, back), load, own
        self.send, self.recv, self.ssem, self.rsem = send, recv, ssem, rsem
        self.long = n // 2
        self.started = []

    def hops(self, unit, way):
        return self.long if unit % 2 == way else self.n - 1 - self.long

    def slot(self, unit, way, s):
        return s if unit % 2 == way else self.long + s

    def copy(self, unit, way, s):
        if s == 0:
            src = self.send.at[unit, way]
        else:
            src = self.recv.at[unit, self.slot(unit, way, s - 1)]
        k = self.slot(unit, way, s)
        return pltpu.make_async_remote_copy(
            src_ref=src, dst_ref=self.recv.at[unit, k], send_sem=self.ssem.at[unit, k], recv_sem=self.rsem.at[unit, k],
            device_id=self.devs[way], device_id_type=MESH)

    def at(self, shift):
        return lax.rem(self.pos + (shift + 2 * self.n), self.n)

    def go(self, unit, way, s):
        cp = self.copy(unit, way, s)
        cp.start()
        self.started.append(cp)

    def start(self, unit):
        for way in (unit % 2, 1 - unit % 2):
            far = self.hops(unit, way)
            q = self.at(far if way == 0 else -far)

            def body(i, _, way=way, q=q):
                self.send[unit, way, i] = self.load(unit, q, i).astype(BF16)
                return 0

            lax.fori_loop(0, self.send.shape[2], body, 0)
            self.go(unit, way, 0)

    def step(self, unit, s):
        last = True
        for way in (unit % 2, 1 - unit % 2):
            far = self.hops(unit, way)
            if s < far:
                self.copy(unit, way, s).wait_recv()
            if s < far - 1:
                last = False
                q = self.at(far - 1 - s if way == 0 else 1 + s - far)
                k = self.slot(unit, way, s)

                def body(i, _, q=q, k=k):
                    self.recv[unit, k, i] = (self.recv[unit, k, i].astype(F32) + self.load(unit, q, i)).astype(BF16)
                    return 0

                lax.fori_loop(0, self.send.shape[2], body, 0)
                self.go(unit, way, s + 1)
        if last:
            k0 = self.slot(unit, 0, self.hops(unit, 0) - 1)
            k1 = self.slot(unit, 1, self.hops(unit, 1) - 1)

            def total(i, _):
                v = self.load(unit, self.pos, i) + self.recv[unit, k0, i].astype(F32) + self.recv[unit, k1, i].astype(F32)
                self.own(unit, i, v)
                return 0

            lax.fori_loop(0, self.send.shape[2], total, 0)

    def finish(self):
        for cp in self.started:
            cp.wait_send()


def kernel(scale, inv_ref, col_ref, x_ref, w_ref, ct_ref, dx_ref, wg_ref,
           s_a, s_b, s_c, r_a, r_b, r_c, own_pre, slope, x_row, x_t, part, two_z, two_x, done,
           z_send, z_recv, x_send, x_recv, u_send, u_recv, v_send, v_recv, y_send, y_recv,
           fs, fr, zss, zrs, xss, xrs, uss, urs, vss, vrs, yss, yrs):
    d = lax.axis_index("dp")
    t = lax.axis_index("tensor")
    x, z, ylo = lax.rem(d, 4), lax.rem(d // 4, 8), d // 32
    yhi, core = t // 2, lax.rem(t, 2)

    def at(xx, zz, yy):
        return ((yy * 8 + zz) * 4 + xx, t)

    core_dev = (d, yhi * 2 + 1 - core)
    far_dev = (d, (1 - yhi) * 2 + core)
    y_dev = at(x, z, 1 - ylo)
    zp, zm = at(x, lax.rem(z + 1, 8), ylo), at(x, lax.rem(z + 7, 8), ylo)
    xp, xm = at(lax.rem(x + 1, 4), z, ylo), at(lax.rem(x + 3, 4), z, ylo)

    barrier = pltpu.get_barrier_semaphore()
    for dev in (core_dev, far_dev, y_dev, zp, zm, xp, xm):
        pl.semaphore_signal(barrier, inc=1, device_id=dev, device_id_type=MESH)
    pl.semaphore_wait(barrier, 7)

    tok = x_ref.shape[0]
    x_t[...] = jnp.zeros_like(x_t)
    slope[:, tok:, :] = jnp.zeros((48, slope.shape[1] - tok, 128), BF16)

    for r in range(24):
        x_row[r] = x_ref[:, 128 * r:128 * r + 128]

    def pre_col(c):
        acc = None
        for gp in range(3):
            i0, i1 = 96 * gp + c, 96 * gp + 48 + c
            b0, b1 = inv_ref[0, i0], inv_ref[0, i1]
            r0, r1 = inv_ref[1, i0], inv_ref[1, i1]
            lhs = jnp.concatenate([x_row[r0], x_row[r1]], axis=1)
            rhs = jnp.concatenate([w_ref[b0], w_ref[b1]], axis=0)
            term = jnp.dot(lhs, rhs, preferred_element_type=F32)
            acc = term if acc is None else acc + term
        return acc

    q_a, q_b, q_c, q_d = (1 - yhi) * 2 + 1 - core, (1 - yhi) * 2 + core, yhi * 2 + 1 - core, t

    def piece(kind, src, dst, p, dev):
        return pltpu.make_async_remote_copy(
            src_ref=src, dst_ref=dst, send_sem=fs.at[kind, p], recv_sem=fr.at[kind, p], device_id=dev, device_id_type=MESH)

    def copy_a(p):
        return piece(0, s_a.at[pl.ds(4 * p, 4)], r_a.at[pl.ds(4 * p, 4)], p, core_dev)

    def copy_b(p):
        return piece(1, s_b.at[pl.ds(4 * p, 4)], r_b.at[pl.ds(4 * p, 4)], p, far_dev)

    def copy_c(p):
        return piece(2, s_c.at[pl.ds(4 * p, 4)], r_c.at[pl.ds(4 * p, 4)], p, core_dev)

    def slope_copy(kind, quarter, p, dev):
        ref = slope.at[pl.ds(quarter * 12 + 4 * p, 4), pl.ds(0, tok)]
        return piece(kind, ref, ref, p, dev)

    def part_a(p, _):
        def col(j, _):
            s_a[4 * p + j] = pre_col(q_a * 12 + 4 * p + j).astype(BF16)
            return 0

        lax.fori_loop(0, 4, col, 0)
        copy_a(p).start()
        return 0

    def part_b(p, _):
        copy_a(p).wait_recv()

        def col(j, _):
            s_b[4 * p + j] = (pre_col(q_b * 12 + 4 * p + j) + r_a[4 * p + j].astype(F32)).astype(BF16)
            return 0

        lax.fori_loop(0, 4, col, 0)
        copy_b(p).start()
        return 0

    def part_c(p, _):
        def col(j, _):
            s_c[4 * p + j] = pre_col(q_c * 12 + 4 * p + j).astype(BF16)
            return 0

        lax.fori_loop(0, 4, col, 0)
        copy_c(p).start()
        return 0

    def part_d(p, _):
        copy_c(p).wait_recv()

        def col(j, _):
            own_pre[4 * p + j] = pre_col(q_d * 12 + 4 * p + j) + r_c[4 * p + j].astype(F32)
            return 0

        lax.fori_loop(0, 4, col, 0)
        return 0

    lax.fori_loop(0, 3, part_a, 0)
    lax.fori_loop(0, 3, part_b, 0)
    lax.fori_loop(0, 3, part_c, 0)
    lax.fori_loop(0, 3, part_d, 0)

    def turn(r, _):
        x_t[r, :, 0:tok] = x_row[r].T
        return 0

    lax.fori_loop(0, 24, turn, 0)

    def part_s(p, _):
        copy_b(p).wait_recv()

        def col(j, _):
            i = 4 * p + j
            pre = own_pre[i] + r_b[i].astype(F32)
            up = ct_ref[:, pl.ds(pl.multiple_of(i * 128, 128), 128)].astype(F32)
            slope[q_d * 12 + i, 0:tok, :] = (up * gelu_slope(pre)).astype(BF16)
            return 0

        lax.fori_loop(0, 4, col, 0)
        slope_copy(3, q_d, p, far_dev).start()
        slope_copy(4, q_d, p, core_dev).start()
        return 0

    def part_f(p, _):
        slope_copy(3, q_b, p, far_dev).wait_recv()
        slope_copy(5, q_b, p, core_dev).start()
        return 0

    def part_g(p, _):
        slope_copy(4, q_c, p, core_dev).wait_recv()
        slope_copy(5, q_a, p, core_dev).wait_recv()
        return 0

    lax.fori_loop(0, 3, part_s, 0)
    lax.fori_loop(0, 3, part_f, 0)
    lax.fori_loop(0, 3, part_g, 0)

    def weight_rows(r, _):
        xt = x_t[r]
        for kp in range(6):
            c0, c1 = col_ref[r * 12 + 2 * kp], col_ref[r * 12 + 2 * kp + 1]
            rhs = jnp.concatenate([slope[c0], slope[c1]], axis=1)
            g = jnp.dot(xt, rhs, preferred_element_type=F32)
            part[r, pl.ds(256 * kp, 128), :] = g[:, :128]
            part[r, pl.ds(256 * kp + 128, 128), :] = g[:, 128:]
        return 0

    def input_rows(r, _):
        acc = None
        for kp in range(6):
            b = r * 12 + 2 * kp
            c0, c1 = col_ref[b], col_ref[b + 1]
            lhs = jnp.concatenate([slope[c0], slope[c1]], axis=1)[0:tok]
            rhs = jnp.concatenate([w_ref[b], w_ref[b + 1]], axis=1)
            term = lax.dot_general(lhs, rhs, (((1,), (1,)), ((), ())), preferred_element_type=F32)
            acc = term if acc is None else acc + term
        dx_ref[:, pl.ds(pl.multiple_of(r * 128, 128), 128)] = acc.astype(BF16)
        return 0

    def load_z(unit, q, i):
        h, u = unit // 2, unit % 2
        return part[6 * h + i, pl.ds(pl.multiple_of((u * 8 + q) * 96, 96), 96), :]

    def own_z(unit, i, v):
        two_z[unit, i] = v

    def load_x(unit, q, i):
        h, u = unit // 2, unit % 2
        base = pl.multiple_of(u * 768 + q * 24, 24)
        return jnp.concatenate([part[12 + 6 * h + i, pl.ds(base + 96 * k, 24), :] for k in range(8)], axis=0)

    def own_x(unit, i, v):
        two_x[unit, i] = v.reshape(8, 24, 128)

    def load_u(unit, q, i):
        return two_x[unit, :, q].reshape(144, 128)

    def own_u(unit, i, v):
        done[1, unit // 2, unit % 2] = v

    def load_v(unit, q, i):
        return two_z[unit, :, pl.ds(pl.multiple_of(q * 24, 24), 24), :].reshape(144, 128)

    def own_v(unit, i, v):
        done[0, unit // 2, unit % 2] = v

    rings = {
        "z": Ring(8, z, zp, zm, load_z, own_z, z_send, z_recv, zss, zrs),
        "x": Ring(4, x, xp, xm, load_x, own_x, x_send, x_recv, xss, xrs),
        "u": Ring(8, z, zp, zm, load_u, own_u, u_send, u_recv, uss, urs),
        "v": Ring(4, x, xp, xm, load_v, own_v, v_send, v_recv, vss, vrs),
    }

    def y_copy(k):
        return pltpu.make_async_remote_copy(
            src_ref=y_send.at[k], dst_ref=y_recv.at[k], send_sem=yss.at[k], recv_sem=yrs.at[k], device_id=y_dev, device_id_type=MESH)

    row = 0
    for kind, unit, s in ORDER:
        if kind == "W":
            lax.fori_loop(6 * unit, 6 * unit + 6, weight_rows, 0)
        elif kind == "D":
            lax.fori_loop(row, row + unit, input_rows, 0)
            row += unit
        elif kind == "ys":
            y_send[unit] = done[unit // 2, unit % 2, 1 - ylo].astype(BF16)
            y_copy(unit).start()
        elif kind == "yt":
            y_copy(unit).wait_recv()
            v = (done[unit // 2, unit % 2, ylo] + y_recv[unit].astype(F32)) * scale
            wg_ref[pl.ds(6 * unit, 6)] = v.reshape(6, 24, 128)
        elif kind[1] == "s":
            rings[kind[0]].start(unit)
        else:
            rings[kind[0]].step(unit, s)
    assert row == 24

    def drain(p, _):
        copy_a(p).wait_send()
        copy_b(p).wait_send()
        copy_c(p).wait_send()
        slope_copy(3, q_d, p, far_dev).wait_send()
        slope_copy(4, q_d, p, core_dev).wait_send()
        slope_copy(5, q_b, p, core_dev).wait_send()
        return 0

    lax.fori_loop(0, 3, drain, 0)
    for ring in rings.values():
        ring.finish()
    for k in range(4):
        y_copy(k).wait_send()


def on_device(features, weights, block_cols, cotangent):
    tok, width = features.shape
    rows = weights.shape[1]
    w_blocks = weights.reshape(12, 128, rows, 128).transpose(2, 0, 1, 3).reshape(rows * 12, 128, 128)
    flat = block_cols.reshape(rows * 12)
    grouped = block_cols.reshape(rows // 4, 48)
    hit = grouped[:, :, None] == jnp.arange(48, dtype=jnp.int32)[None, None, :]
    block = jnp.arange(rows * 12, dtype=jnp.int32).reshape(rows // 4, 48)
    inv = jnp.stack([
        jnp.sum(jnp.where(hit, block[:, :, None], 0), axis=1).reshape(-1),
        jnp.sum(jnp.where(hit, (block // 12)[:, :, None], 0), axis=1).reshape(-1),
    ])
    scale = float(tok * lax.axis_size("dp")) ** (-0.5)
    vmem = pl.BlockSpec(memory_space=pltpu.VMEM)
    smem = pl.BlockSpec(memory_space=pltpu.SMEM)
    dma = pltpu.SemaphoreType.DMA
    quarter = pltpu.VMEM((12, tok, 128), BF16)
    dx, wg = pl.pallas_call(
        functools.partial(kernel, scale),
        out_shape=(jax.ShapeDtypeStruct((tok, width), BF16), jax.ShapeDtypeStruct((rows, 24, 128), F32)),
        in_specs=[smem, smem, vmem, vmem, vmem],
        out_specs=(vmem, vmem),
        scratch_shapes=[
            quarter, quarter, quarter, quarter, quarter, quarter,
            pltpu.VMEM((12, tok, 128), F32),
            pltpu.VMEM((48, 256, 128), BF16),
            pltpu.VMEM((rows, tok, 128), BF16),
            pltpu.VMEM((rows, 128, 256), BF16),
            pltpu.VMEM((rows, 1536, 128), F32),
            pltpu.VMEM((4, 6, 96, 128), F32),
            pltpu.VMEM((4, 6, 8, 24, 128), F32),
            pltpu.VMEM((2, 2, 2, 144, 128), F32),
            pltpu.VMEM((4, 2, 6, 96, 128), BF16),
            pltpu.VMEM((4, 7, 6, 96, 128), BF16),
            pltpu.VMEM((4, 2, 6, 192, 128), BF16),
            pltpu.VMEM((4, 3, 6, 192, 128), BF16),
            pltpu.VMEM((4, 2, 1, 144, 128), BF16),
            pltpu.VMEM((4, 7, 1, 144, 128), BF16),
            pltpu.VMEM((4, 2, 1, 144, 128), BF16),
            pltpu.VMEM((4, 3, 1, 144, 128), BF16),
            pltpu.VMEM((4, 144, 128), BF16),
            pltpu.VMEM((4, 144, 128), BF16),
            dma((6, 3)), dma((6, 3)),
            dma((4, 7)), dma((4, 7)),
            dma((4, 3)), dma((4, 3)),
            dma((4, 7)), dma((4, 7)),
            dma((4, 3)), dma((4, 3)),
            dma((4,)), dma((4,)),
        ],
        compiler_params=pltpu.CompilerParams(
            collective_id=0, has_side_effects=True, vmem_limit_bytes=63 * 2**20),
        name="block_grads",
    )(inv, flat, features, w_blocks, cotangent)
    return dx, wg.transpose(1, 0, 2)


def solution(mesh):
    return jax.shard_map(
        on_device,
        mesh=mesh,
        in_specs=(P("dp", "tensor"), P(None, "tensor", None), P("tensor", None), P("dp", "tensor")),
        out_specs=(P("dp", "tensor"), P("dp", "tensor", None)),
        check_vma=False,
    )
```

```python
import functools

import jax
import jax.numpy as jnp
from jax import lax
from jax.experimental import pallas as pl
from jax.experimental.pallas import tpu as pltpu
from jax.sharding import PartitionSpec as P

MESH = pl.DeviceIdType.MESH
F32 = jnp.float32
BF16 = jnp.bfloat16
gelu_coef = 0.7978845608

GROUPS = "zzxX"
ROWS = 3

ORDER = (
    ("W", 1), ("start", 2, 1), ("start", 3, 1), ("W", 3), ("y1s", 3), ("W", 2), ("start", 4, 1), ("start", 5, 1), ("step", 2, 1, 0),
    ("step", 3, 1, 0), ("W", 0), ("start", 0, 1), ("start", 1, 1), ("D", 1), ("step", 2, 1, 1), ("D", 3), ("step", 3, 1, 1), ("D", 3),
    ("step", 0, 1, 0), ("step", 4, 1, 0), ("start", 4, 2), ("step", 1, 1, 0), ("D", 3), ("step", 2, 1, 2), ("D", 3), ("y1t", 3), ("start", 6, 1),
    ("step", 3, 1, 2), ("step", 0, 1, 1), ("step", 5, 1, 0), ("step", 4, 2, 0), ("start", 5, 2), ("D", 1), ("step", 1, 1, 1), ("D", 2),
    ("step", 2, 1, 3), ("step", 3, 1, 3), ("start", 2, 2), ("start", 3, 2), ("D", 3), ("step", 0, 1, 2), ("D", 1), ("step", 4, 2, 1), ("D", 1),
    ("step", 5, 2, 0), ("D", 2), ("step", 6, 1, 0), ("start", 6, 2), ("step", 1, 1, 2), ("step", 2, 2, 0), ("step", 3, 2, 0), ("ys", 1),
    ("step", 0, 1, 3), ("start", 0, 2), ("D", 1), ("step", 4, 2, 2), ("step", 5, 2, 1), ("step", 6, 2, 0), ("xl", 1), ("step", 1, 1, 3),
    ("step", 0, 2, 0), ("start", 1, 2), ("step", 4, 2, 3), ("step", 5, 2, 2), ("step", 6, 2, 1), ("out", 1), ("step", 1, 2, 0), ("ys", 0),
    ("step", 5, 2, 3), ("ys", 2), ("step", 6, 2, 2), ("xl", 0), ("xl", 2), ("step", 6, 2, 3), ("xl", 3), ("out", 0), ("out", 2), ("out", 3),
)

UNITS = [(g, u) for g, a in enumerate(GROUPS) for u in ((None,) if a.isupper() else (0, 1))]


def gelu_slope(v):
    th = jnp.tanh(gelu_coef * (v + 0.044715 * v * v * v))
    return 0.5 * (1.0 + th) + 0.5 * v * (1.0 - th * th) * gelu_coef * (1.0 + 0.134145 * v * v)


class Ring:
    def __init__(self, n, pos, ahead, back, units, load, own, send, recv, ssem, rsem):
        self.n, self.pos, self.devs, self.load, self.own = n, pos, (ahead, back), load, own
        self.send, self.recv, self.ssem, self.rsem = send, recv, ssem, rsem
        self.long = n // 2
        self.index = {unit: i for i, unit in enumerate(units)}
        self.started = []

    def ways(self, unit):
        g, u = UNITS[unit]
        first = (g if u is None else u) % 2
        return ((first, self.long, 0), (1 - first, self.n - 1 - self.long, self.long))

    def go(self, unit, way, slot, s):
        j = self.index[unit]
        src = self.send.at[j, way % self.send.shape[1]] if s == 0 else self.recv.at[j, slot + s - 1]
        cp = pltpu.make_async_remote_copy(
            src_ref=src, dst_ref=self.recv.at[j, slot + s], send_sem=self.ssem.at[j, slot + s], recv_sem=self.rsem.at[j, slot + s],
            device_id=self.devs[way], device_id_type=MESH)
        cp.start()
        self.started.append(cp)

    def arrived(self, unit, way, slot, s):
        j = self.index[unit]
        ref = self.recv.at[j, slot + s]
        pltpu.make_async_remote_copy(
            src_ref=ref, dst_ref=ref, send_sem=self.ssem.at[j, slot + s], recv_sem=self.rsem.at[j, slot + s],
            device_id=self.devs[way], device_id_type=MESH).wait_recv()

    def at(self, shift):
        return lax.rem(self.pos + (shift + 2 * self.n), self.n)

    def start(self, unit):
        j = self.index[unit]
        for way, far, slot in self.ways(unit):
            if far == 0:
                continue
            q = self.at(far if way == 0 else -far)

            def body(i, _, way=way, q=q):
                self.send[j, way % self.send.shape[1], i] = self.load(unit, q, i).astype(BF16)
                return 0

            lax.fori_loop(0, self.send.shape[2], body, 0)
            self.go(unit, way, slot, 0)

    def step(self, unit, s):
        j = self.index[unit]
        for way, far, slot in self.ways(unit):
            if s < far:
                self.arrived(unit, way, slot, s)
            if s < far - 1:
                q = self.at(far - 1 - s if way == 0 else 1 + s - far)

                def body(i, _, q=q, k=slot + s):
                    self.recv[j, k, i] = (self.recv[j, k, i].astype(F32) + self.load(unit, q, i)).astype(BF16)
                    return 0

                lax.fori_loop(0, self.send.shape[2], body, 0)
                self.go(unit, way, slot, s + 1)
        if s == self.long - 1:
            ends = [slot + far - 1 for _, far, slot in self.ways(unit) if far]

            def total(i, _):
                v = self.load(unit, self.pos, i)
                for k in ends:
                    v = v + self.recv[j, k, i].astype(F32)
                self.own(unit, i, v)
                return 0

            lax.fori_loop(0, self.send.shape[2], total, 0)

    def finish(self):
        for cp in self.started:
            cp.wait_send()


def kernel(scale, meta_ref, x_hbm, w_hbm, ct_hbm, dx_ref, wg_ref,
           w_ref, raw, ct_ref, s_a, s_b, s_c, r_a, r_b, r_c, slope, x_row, x_in, x_t, part, two_z, two_x, done, last, wg_rows,
           z_send, z_recv, x_send, x_recv, u_send, u_recv, v_send, v_recv, y_send, y_recv, f_send, f_recv, n_send,
           xl, wl, cl, fs, fr, xis, xir, zss, zrs, xss, xrs, uss, urs, vss, vrs, yss, yrs, fss, frs, nss, nrs):
    d = lax.axis_index("dp")
    t = lax.axis_index("tensor")
    x, z, ylo = lax.rem(d, 4), lax.rem(d // 4, 8), d // 32
    yhi, core = t // 2, lax.rem(t, 2)

    def at(xx, zz, yy):
        return ((yy * 8 + zz) * 4 + xx, t)

    core_dev = (d, yhi * 2 + 1 - core)
    far_dev = (d, (1 - yhi) * 2 + core)
    y_dev = at(x, z, 1 - ylo)
    zp, zm = at(x, lax.rem(z + 1, 8), ylo), at(x, lax.rem(z + 7, 8), ylo)
    xhi, xlo = x // 2, lax.rem(x, 2)
    x_far, x_dev = at(lax.rem(x + 2, 4), z, ylo), at(x + 1 - 2 * xlo, z, ylo)
    base = 12 * xlo

    barrier = pltpu.get_barrier_semaphore()
    for dev in (core_dev, far_dev, y_dev, zp, zm, x_far, x_dev):
        pl.semaphore_signal(barrier, inc=1, device_id=dev, device_id_type=MESH)

    tok = x_hbm.shape[0]

    def x_copy(r):
        return pltpu.make_async_copy(x_hbm.at[:, pl.ds(128 * r, 128)], x_row.at[r], xl.at[r])

    def w_copy(k):
        return pltpu.make_async_copy(w_hbm.at[pl.ds(128 * k, 128)], raw.at[k], wl.at[k])

    ct_copy = pltpu.make_async_copy(ct_hbm, ct_ref, cl)
    for k in range(12):
        w_copy(k).start()
    for r in range(24):
        x_copy(r).start()
    ct_copy.start()
    x_t[...] = jnp.zeros_like(x_t)
    slope[:, tok:256, :] = jnp.zeros((48, 256 - tok, 128), BF16)
    slope[:, 256 + tok:, :] = jnp.zeros((48, 256 - tok, 128), BF16)

    for k in range(12):
        w_copy(k).wait()
        for half in range(2):
            part[half] = raw[k, 64 * half:64 * half + 64].astype(F32).reshape(1536, 128)

            def sort_rows(r, _, k=k, half=half):
                w_ref[r * 12 + k, 64 * half:64 * half + 64, :] = part[half, pl.ds(r, 64, stride=24), :].astype(BF16)
                return 0

            lax.fori_loop(0, 24, sort_rows, 0, unroll=4)
    for r in range(24):
        x_copy(r).wait()

    def pre_col(c):
        acc = None
        for gp in range(3):
            b0, b1 = meta_ref[2 * gp, c], meta_ref[2 * gp + 1, c]
            r0, r1 = lax.div(b0, 12), lax.div(b1, 12)
            lhs = jnp.concatenate([x_row[r0], x_row[r1]], axis=1)
            rhs = jnp.concatenate([w_ref[b0], w_ref[b1]], axis=0)
            term = jnp.dot(lhs, rhs, preferred_element_type=F32)
            acc = term if acc is None else acc + term
        return acc

    q_a, q_b, q_c, q_d = (1 - yhi) * 2 + 1 - core, (1 - yhi) * 2 + core, yhi * 2 + 1 - core, t

    def piece(kind, src, dst, p, dev):
        return pltpu.make_async_remote_copy(
            src_ref=src, dst_ref=dst, send_sem=fs.at[kind, p], recv_sem=fr.at[kind, p], device_id=dev, device_id_type=MESH)

    def copy_a(p):
        return piece(0, s_a.at[pl.ds(2 * p, 2)], r_a.at[pl.ds(2 * p, 2)], p, core_dev)

    def copy_b(p):
        return piece(1, s_b.at[pl.ds(2 * p, 2)], r_b.at[pl.ds(2 * p, 2)], p, far_dev)

    def copy_c(p):
        return piece(2, s_c.at[pl.ds(2 * p, 2)], r_c.at[pl.ds(2 * p, 2)], p, core_dev)

    def slope_copy(kind, quarter, p, dev, src=0, dst=0):
        cols = pl.ds(quarter * 12 + 2 * p, 2)
        return piece(kind, slope.at[cols, pl.ds(src, tok)], slope.at[cols, pl.ds(dst, tok)], p, dev)

    def far_copy(p):
        return slope_copy(3, q_d, p, far_dev)

    def core_copy(i, p):
        return slope_copy((4, 5, 8, 9)[i], q_b if i % 2 else q_d, p, core_dev, i // 2 * 256, i // 2 * 256)

    def x_copy_out(i, p):
        return slope_copy(6 + i, q_b if i else q_d, p, x_dev, 0, 256)

    x_move = pltpu.make_async_remote_copy(
        src_ref=x_row.at[pl.ds(12 - base, 12)], dst_ref=x_in, send_sem=xis, recv_sem=xir, device_id=x_dev, device_id_type=MESH)

    def part_a(p, _):
        for i in (2 * p, 2 * p + 1):
            s_a[i] = pre_col(q_a * 12 + i).astype(BF16)
        copy_a(p).start()
        return 0

    def part_b(p, _):
        copy_a(p).wait_recv()
        for i in (2 * p, 2 * p + 1):
            s_b[i] = (pre_col(q_b * 12 + i) + r_a[i].astype(F32)).astype(BF16)
        copy_b(p).start()
        return 0

    def part_ab(p, _):
        part_a(p + 1, 0)
        return part_b(p, 0)

    def part_c(p, _):
        for i in (2 * p, 2 * p + 1):
            s_c[i] = pre_col(q_c * 12 + i).astype(BF16)
        copy_c(p).start()
        return 0

    def part_d(p, _):
        copy_c(p).wait_recv()
        for i in (2 * p, 2 * p + 1):
            part[p, pl.ds(tok * (i - 2 * p), tok), :] = pre_col(q_d * 12 + i) + r_c[i].astype(F32)
        return 0

    pl.semaphore_wait(barrier, 7)
    x_move.start()
    part_a(0, 0)
    lax.fori_loop(0, 5, part_ab, 0)
    part_b(5, 0)
    lax.fori_loop(0, 6, part_c, 0)
    lax.fori_loop(0, 6, part_d, 0)

    def turn(r, _):
        x_t[r, :, 0:tok] = x_row[base + r].T
        x_t[r, :, 256:256 + tok] = x_in[r].T
        return 0

    def part_s(p, _):
        copy_b(p).wait_recv()
        for i in (2 * p, 2 * p + 1):
            pre = part[p, pl.ds(tok * (i - 2 * p), tok), :] + r_b[i].astype(F32)
            up = ct_ref[:, pl.ds(pl.multiple_of(i * 128, 128), 128)].astype(F32)
            slope[q_d * 12 + i, 0:tok, :] = (up * gelu_slope(pre)).astype(BF16)
        far_copy(p).start()
        core_copy(0, p).start()
        x_copy_out(0, p).start()
        return 0

    def relay(p, _):
        slope_copy(6, q_d, p, x_dev, 256, 256).wait_recv()
        core_copy(2, p).start()
        slope_copy(3, q_b, p, far_dev).wait_recv()
        x_copy_out(1, p).start()
        core_copy(1, p).start()
        return 0

    def relay_last(p, _):
        slope_copy(7, q_b, p, x_dev, 256, 256).wait_recv()
        core_copy(3, p).start()
        return 0

    def relay_both(p, _):
        relay(p, 0)
        return relay_last(p - 2, 0)

    def gathered(p, _):
        slope_copy(4, q_c, p, core_dev).wait_recv()
        slope_copy(5, q_a, p, core_dev).wait_recv()
        slope_copy(8, q_c, p, core_dev, 256, 256).wait_recv()
        slope_copy(9, q_a, p, core_dev, 256, 256).wait_recv()
        return 0

    ct_copy.wait()
    lax.fori_loop(0, 6, part_s, 0)
    x_move.wait_recv()
    lax.fori_loop(0, 12, turn, 0)
    lax.fori_loop(0, 2, relay, 0)
    lax.fori_loop(2, 6, relay_both, 0)
    lax.fori_loop(4, 6, relay_last, 0)
    lax.fori_loop(0, 6, gathered, 0)

    def column(r, slot):
        return meta_ref[6 + lax.div(r, 4), lax.rem(r, 4) * 12 + slot]

    def weight_rows(j, _):
        xt = x_t[j]
        for kp in range(6):
            c0, c1 = column(base + j, 2 * kp), column(base + j, 2 * kp + 1)
            rhs = jnp.concatenate([slope[c0], slope[c1]], axis=1)
            g = jnp.dot(xt, rhs, preferred_element_type=F32)
            part[j, pl.ds(256 * kp, 128), :] = g[:, :128]
            part[j, pl.ds(256 * kp + 128, 128), :] = g[:, 128:]
        return 0

    def input_rows(r, _):
        acc = None
        for kp in range(6):
            b = r * 12 + 2 * kp
            c0, c1 = column(r, 2 * kp), column(r, 2 * kp + 1)
            lhs = jnp.concatenate([slope[c0], slope[c1]], axis=1)[0:tok]
            rhs = jnp.concatenate([w_ref[b], w_ref[b + 1]], axis=1)
            term = lax.dot_general(lhs, rhs, (((1,), (1,)), ((), ())), preferred_element_type=F32)
            acc = term if acc is None else acc + term
        dx_ref[:, pl.ds(pl.multiple_of(r * 128, 128), 128)] = acc.astype(BF16)
        return 0

    z_units = [i for i, (g, _) in enumerate(UNITS) if GROUPS[g] in "zZ"]
    x_units = [i for i, (g, _) in enumerate(UNITS) if GROUPS[g] in "xX"]

    def half(unit):
        u = UNITS[unit][1]
        return ylo if u is None else u

    def load_z(unit, q, i):
        return part[ROWS * UNITS[unit][0] + i, pl.ds(pl.multiple_of(half(unit) * 768 + q * 96, 32), 96), :]

    def own_z(unit, i, v):
        two_z[z_units.index(unit), i] = v

    def load_x(unit, q, i):
        first = pl.multiple_of(half(unit) * 768 + q * 48, 16)
        row = ROWS * UNITS[unit][0] + i
        return jnp.concatenate([part[row, pl.ds(first + 96 * k, 48), :] for k in range(8)], axis=0)

    def own_x(unit, i, v):
        two_x[x_units.index(unit), i] = v.reshape(8, 48, 128)

    def load_u(unit, q, i):
        return two_x[x_units.index(unit), :, q].reshape(ROWS * 48, 128)

    def load_v(unit, q, i):
        return two_z[z_units.index(unit), :, pl.ds(pl.multiple_of(q * 48, 16), 48), :].reshape(ROWS * 48, 128)

    def own_last(unit, i, v):
        done[unit] = v

    stages = [
        {"z": Ring(8, z, zp, zm, z_units, load_z, own_z, z_send, z_recv, zss, zrs),
         "x": Ring(2, xhi, x_far, x_far, x_units, load_x, own_x, x_send, x_recv, xss, xrs)},
        {"x": Ring(8, z, zp, zm, x_units, load_u, own_last, u_send, u_recv, uss, urs),
         "z": Ring(2, xhi, x_far, x_far, z_units, load_v, own_last, v_send, v_recv, vss, vrs)},
    ]

    def y_copy(g):
        return pltpu.make_async_remote_copy(
            src_ref=y_send.at[g], dst_ref=y_recv.at[g], send_sem=yss.at[g], recv_sem=yrs.at[g], device_id=y_dev, device_id_type=MESH)

    firsts = [g for g, a in enumerate(GROUPS) if a.isupper()]

    def first_copy(g):
        i = firsts.index(g)
        return pltpu.make_async_remote_copy(
            src_ref=f_send.at[i], dst_ref=f_recv.at[i], send_sem=fss.at[i], recv_sem=frs.at[i], device_id=y_dev, device_id_type=MESH)

    def next_copy(g, owner):
        return pltpu.make_async_remote_copy(
            src_ref=n_send.at[g], dst_ref=wg_rows.at[pl.ds(12 * owner + ROWS * g, ROWS)], send_sem=nss.at[g], recv_sem=nrs.at[g],
            device_id=x_dev, device_id_type=MESH)

    row = 0
    waits = []
    for kind, *what in ORDER:
        if kind == "D":
            lax.fori_loop(row, row + what[0], input_rows, 0)
            row += what[0]
            continue
        if kind in ("start", "step"):
            unit, stage = what[:2]
            ring = stages[stage - 1][GROUPS[UNITS[unit][0]].lower()]
            if kind == "start":
                ring.start(unit)
            else:
                ring.step(unit, what[2])
            continue
        g = what[0]
        unit = [i for i, u in enumerate(UNITS) if u[0] == g][0]
        if kind == "W":
            lax.fori_loop(ROWS * g, ROWS * g + ROWS, weight_rows, 0)
        elif kind == "y1s":
            def give(i, _, g=g):
                f_send[firsts.index(g), i] = part[ROWS * g + i, pl.ds(pl.multiple_of((1 - ylo) * 768, 768), 768), :].astype(BF16)
                return 0

            lax.fori_loop(0, ROWS, give, 0)
            first_copy(g).start()
            waits.append(first_copy(g))
        elif kind == "y1t":
            first_copy(g).wait_recv()

            def take(i, _, g=g):
                rows = pl.ds(pl.multiple_of(ylo * 768, 768), 768)
                part[ROWS * g + i, rows, :] = part[ROWS * g + i, rows, :] + f_recv[firsts.index(g), i].astype(F32)
                return 0

            lax.fori_loop(0, ROWS, take, 0)
        elif kind == "ys":
            y_send[g] = done[unit + 1 - ylo].astype(BF16)
            y_copy(g).start()
            waits.append(y_copy(g))
        elif kind == "xl":
            if UNITS[unit][1] is None:
                v = done[unit]
            else:
                y_copy(g).wait_recv()
                v = done[unit + ylo] + y_recv[g].astype(F32)
            last[g] = (v * scale).reshape(ROWS, 48, 128)
            wg_rows[pl.ds(base + ROWS * g, ROWS)] = last[g, :, pl.ds(pl.multiple_of(24 * xlo, 8), 24), :]
            n_send[g] = last[g, :, pl.ds(pl.multiple_of(24 - 24 * xlo, 8), 24), :]
            next_copy(g, xlo).start()
            waits.append(next_copy(g, xlo))
        else:
            next_copy(g, 1 - xlo).wait_recv()
    assert row == 24
    for r in range(24):
        wg_ref[:, r, :] = wg_rows[r]

    def drain(p, _):
        copy_a(p).wait_send()
        copy_b(p).wait_send()
        copy_c(p).wait_send()
        far_copy(p).wait_send()
        for i in range(4):
            core_copy(i, p).wait_send()
        for i in range(2):
            x_copy_out(i, p).wait_send()
        return 0

    lax.fori_loop(0, 6, drain, 0)
    x_move.wait_send()
    for stage in stages:
        for ring in stage.values():
            ring.finish()
    for cp in waits:
        cp.wait_send()


def on_device(features, weights, block_cols, cotangent):
    tok, width = features.shape
    rows = weights.shape[1]
    row = jnp.arange(rows, dtype=jnp.int32)[:, None, None, None]
    slot = jnp.arange(12, dtype=jnp.int32)[None, :, None, None]
    line = jnp.arange(12, dtype=jnp.int32)[None, None, :, None]
    place = jnp.arange(48, dtype=jnp.int32)[None, None, None, :]
    cols = block_cols[:, :, None, None]
    hit = (row // 4 == line % 6) & (jnp.where(line < 6, cols, row % 4 * 12 + slot) == place)
    meta = jnp.sum(jnp.where(hit, jnp.where(line < 6, row * 12 + slot, cols), 0), axis=(0, 1))
    scale = float(tok * lax.axis_size("dp")) ** (-0.5)
    vmem = pl.BlockSpec(memory_space=pltpu.VMEM)
    smem = pl.BlockSpec(memory_space=pltpu.SMEM)
    any_ = pl.BlockSpec(memory_space=pl.ANY)
    dma = pltpu.SemaphoreType.DMA
    quarter = pltpu.VMEM((12, tok, 128), BF16)
    n_groups = len(GROUPS)
    nz = sum(GROUPS[g] in "zZ" for g, _ in UNITS)
    nx = len(UNITS) - nz
    ny = max(1, sum(a.isupper() for a in GROUPS))
    dx, wg = pl.pallas_call(
        functools.partial(kernel, scale),
        out_shape=(jax.ShapeDtypeStruct((tok, width), BF16), jax.ShapeDtypeStruct((24, rows, 128), F32)),
        in_specs=[smem, any_, any_, any_],
        out_specs=(vmem, vmem),
        scratch_shapes=[
            pltpu.VMEM((rows * 12, 128, 128), BF16),
            pltpu.VMEM((12, 128, rows, 128), BF16),
            pltpu.VMEM((tok, 1536), BF16),
            quarter, quarter, quarter, quarter, quarter, quarter,
            pltpu.VMEM((48, 512, 128), BF16),
            pltpu.VMEM((rows, tok, 128), BF16),
            pltpu.VMEM((12, tok, 128), BF16),
            pltpu.VMEM((12, 128, 512), BF16),
            pltpu.VMEM((12, 1536, 128), F32),
            pltpu.VMEM((nz, ROWS, 96, 128), F32),
            pltpu.VMEM((nx, ROWS, 8, 48, 128), F32),
            pltpu.VMEM((len(UNITS), ROWS * 48, 128), F32),
            pltpu.VMEM((n_groups, ROWS, 48, 128), F32),
            pltpu.VMEM((rows, 24, 128), F32),
            pltpu.VMEM((nz, 2, ROWS, 96, 128), BF16),
            pltpu.VMEM((nz, 7, ROWS, 96, 128), BF16),
            pltpu.VMEM((nx, 1, ROWS, 384, 128), BF16),
            pltpu.VMEM((nx, 1, ROWS, 384, 128), BF16),
            pltpu.VMEM((nx, 2, 1, ROWS * 48, 128), BF16),
            pltpu.VMEM((nx, 7, 1, ROWS * 48, 128), BF16),
            pltpu.VMEM((nz, 1, 1, ROWS * 48, 128), BF16),
            pltpu.VMEM((nz, 1, 1, ROWS * 48, 128), BF16),
            pltpu.VMEM((n_groups, ROWS * 48, 128), BF16),
            pltpu.VMEM((n_groups, ROWS * 48, 128), BF16),
            pltpu.VMEM((ny, ROWS, 768, 128), BF16),
            pltpu.VMEM((ny, ROWS, 768, 128), BF16),
            pltpu.VMEM((n_groups, ROWS, 24, 128), F32),
            dma((rows,)), dma((12,)), dma(()),
            dma((10, 6)), dma((10, 6)),
            dma(()), dma(()),
            dma((nz, 7)), dma((nz, 7)),
            dma((nx, 1)), dma((nx, 1)),
            dma((nx, 7)), dma((nx, 7)),
            dma((nz, 1)), dma((nz, 1)),
            dma((n_groups,)), dma((n_groups,)),
            dma((ny,)), dma((ny,)),
            dma((n_groups,)), dma((n_groups,)),
        ],
        compiler_params=pltpu.CompilerParams(
            collective_id=0, has_side_effects=True, vmem_limit_bytes=62 * 2**20),
        name="block_grads",
    )(meta, features, weights, cotangent)
    return dx, wg


def solution(mesh):
    return jax.shard_map(
        on_device,
        mesh=mesh,
        in_specs=(P("dp", "tensor"), P(None, "tensor", None), P("tensor", None), P("dp", "tensor")),
        out_specs=(P("dp", "tensor"), P("dp", "tensor", None)),
        check_vma=False,
    )
```

```python
import functools

import jax
import jax.numpy as jnp
from jax import lax
from jax.experimental import pallas as pl
from jax.experimental.pallas import tpu as pltpu
from jax.sharding import PartitionSpec as P

MESH = pl.DeviceIdType.MESH
F32 = jnp.float32
BF16 = jnp.bfloat16
gelu_coef = 0.7978845608

GROUPS = "zzxxXZ"
ROWS = 2
COLS = 3
PIECES = 12 // COLS
VIA_X = 3

ORDER = (
    ("W", 3), ("start", 7, 1), ("W", 4), ("y1s", 4), ("start", 6, 1), ("W", 0), ("start", 1, 1), ("start", 0, 1), ("W", 1), ("start", 3, 1),
    ("start", 2, 1), ("W", 2), ("start", 5, 1), ("W", 5), ("y1s", 5), ("step", 1, 1, 0), ("step", 7, 1, 0), ("start", 7, 2), ("D", 1),
    ("step", 0, 1, 0), ("D", 2), ("step", 3, 1, 0), ("D", 1), ("start", 4, 1), ("D", 1), ("step", 2, 1, 0), ("D", 3), ("step", 1, 1, 1), ("D", 1),
    ("step", 6, 1, 0), ("step", 7, 2, 0), ("start", 6, 2), ("D", 2), ("step", 0, 1, 1), ("y1t", 4), ("D", 1), ("start", 8, 1), ("D", 1),
    ("step", 3, 1, 1), ("D", 2), ("step", 2, 1, 1), ("D", 3), ("step", 5, 1, 0), ("step", 1, 1, 2), ("start", 5, 2), ("D", 1), ("step", 7, 2, 1),
    ("D", 1), ("step", 6, 2, 0), ("D", 2), ("step", 0, 1, 2), ("D", 2), ("step", 3, 1, 2), ("step", 4, 1, 0), ("start", 4, 2), ("step", 2, 1, 2),
    ("step", 1, 1, 3), ("y1t", 5), ("start", 9, 1), ("step", 5, 2, 0), ("step", 7, 2, 2), ("step", 6, 2, 1), ("step", 0, 1, 3), ("fs", 0),
    ("step", 3, 1, 3), ("step", 8, 1, 0), ("start", 8, 2), ("step", 4, 2, 0), ("step", 2, 1, 3), ("fs", 1), ("step", 9, 1, 0), ("step", 5, 2, 1),
    ("step", 7, 2, 3), ("step", 6, 2, 2), ("ft", 0), ("step", 8, 2, 0), ("step", 4, 2, 1), ("step", 9, 1, 1), ("ft", 1), ("step", 5, 2, 2),
    ("step", 6, 2, 3), ("fs", 3), ("step", 8, 2, 1), ("step", 4, 2, 2), ("step", 9, 1, 2), ("step", 5, 2, 3), ("step", 8, 2, 2), ("ft", 3),
    ("step", 4, 2, 3), ("fs", 2), ("step", 9, 1, 3), ("fs", 5), ("step", 8, 2, 3), ("fs", 4), ("ft", 2), ("ft", 5), ("ft", 4),
)

UNITS = [(g, u) for g, a in enumerate(GROUPS) for u in ((None,) if a.isupper() else (0, 1))]


def gelu_slope(v):
    th = jnp.tanh(gelu_coef * (v + 0.044715 * v * v * v))
    return 0.5 * (1.0 + th) + 0.5 * v * (1.0 - th * th) * gelu_coef * (1.0 + 0.134145 * v * v)


class Ring:
    def __init__(self, n, pos, ahead, back, units, load, own, send, recv, ssem, rsem):
        self.n, self.pos, self.devs, self.load, self.own = n, pos, (ahead, back), load, own
        self.send, self.recv, self.ssem, self.rsem = send, recv, ssem, rsem
        self.long = n // 2
        self.index = {unit: i for i, unit in enumerate(units)}
        self.started = []

    def ways(self, unit):
        g, u = UNITS[unit]
        first = (g if u is None else u) % 2
        return ((first, self.long, 0), (1 - first, self.n - 1 - self.long, self.long))

    def go(self, unit, way, slot, s):
        j = self.index[unit]
        src = self.send.at[j, way % self.send.shape[1]] if s == 0 else self.recv.at[j, slot + s - 1]
        cp = pltpu.make_async_remote_copy(
            src_ref=src, dst_ref=self.recv.at[j, slot + s], send_sem=self.ssem.at[j, slot + s], recv_sem=self.rsem.at[j, slot + s],
            device_id=self.devs[way], device_id_type=MESH)
        cp.start()
        self.started.append(cp)

    def arrived(self, unit, way, slot, s):
        j = self.index[unit]
        ref = self.recv.at[j, slot + s]
        pltpu.make_async_remote_copy(
            src_ref=ref, dst_ref=ref, send_sem=self.ssem.at[j, slot + s], recv_sem=self.rsem.at[j, slot + s],
            device_id=self.devs[way], device_id_type=MESH).wait_recv()

    def at(self, shift):
        return lax.rem(self.pos + (shift + 2 * self.n), self.n)

    def start(self, unit):
        j = self.index[unit]
        for way, far, slot in self.ways(unit):
            if far == 0:
                continue
            q = self.at(far if way == 0 else -far)

            def body(i, _, way=way, q=q):
                self.send[j, way % self.send.shape[1], i] = self.load(unit, q, i).astype(BF16)
                return 0

            lax.fori_loop(0, self.send.shape[2], body, 0)
            self.go(unit, way, slot, 0)

    def step(self, unit, s):
        j = self.index[unit]
        for way, far, slot in self.ways(unit):
            if s < far:
                self.arrived(unit, way, slot, s)
            if s < far - 1:
                q = self.at(far - 1 - s if way == 0 else 1 + s - far)

                def body(i, _, q=q, k=slot + s):
                    self.recv[j, k, i] = (self.recv[j, k, i].astype(F32) + self.load(unit, q, i)).astype(BF16)
                    return 0

                lax.fori_loop(0, self.send.shape[2], body, 0)
                self.go(unit, way, slot, s + 1)
        if s == self.long - 1:
            ends = [slot + far - 1 for _, far, slot in self.ways(unit) if far]

            def total(i, _):
                v = self.load(unit, self.pos, i)
                for k in ends:
                    v = v + self.recv[j, k, i].astype(F32)
                self.own(unit, i, v)
                return 0

            lax.fori_loop(0, self.send.shape[2], total, 0)

    def finish(self):
        for cp in self.started:
            cp.wait_send()


def kernel(scale, meta_ref, x_hbm, w_hbm, ct_hbm, dx_hbm, wg_ref,
           w_ref, raw, ct_ref, dx_ref, s_a, s_b, s_c, r_a, r_b, r_c, slope, slope_next, x_row, x_in, x_t, part, two_z, two_x, done, wg_rows,
           z_send, z_recv, x_send, x_recv, u_send, u_recv, f_send, f_recv, g_send, g_recv,
           xl, wl, cl, dl, fs, fr, xis, xir, zss, zrs, xss, xrs, uss, urs, fss, frs, gss, grs):
    d = lax.axis_index("dp")
    t = lax.axis_index("tensor")
    x, z, ylo = lax.rem(d, 4), lax.rem(d // 4, 8), d // 32
    yhi, core = t // 2, lax.rem(t, 2)

    def at(xx, zz, yy):
        return ((yy * 8 + zz) * 4 + xx, t)

    core_dev = (d, yhi * 2 + 1 - core)
    far_dev = (d, (1 - yhi) * 2 + core)
    y_dev = at(x, z, 1 - ylo)
    zp, zm = at(x, lax.rem(z + 1, 8), ylo), at(x, lax.rem(z + 7, 8), ylo)
    xhi, xlo = x // 2, lax.rem(x, 2)
    near = {(dx, dy): at(lax.rem(x + dx, 4), z, lax.rem(ylo + dy, 2)) for dx in range(4) for dy in range(2) if dx or dy}
    x_far, x_dev = near[2, 0], at(x + 1 - 2 * xlo, z, ylo)
    pair = {(0, 1): y_dev, (1, 0): x_dev, (1, 1): at(x + 1 - 2 * xlo, z, 1 - ylo)}
    base = 12 * xlo

    barrier = pltpu.get_barrier_semaphore()
    for dev in (core_dev, far_dev, zp, zm, *near.values()):
        pl.semaphore_signal(barrier, inc=1, device_id=dev, device_id_type=MESH)

    tok = x_hbm.shape[0]

    def x_copy(r):
        return pltpu.make_async_copy(x_hbm.at[:, pl.ds(128 * r, 128)], x_row.at[r], xl.at[r])

    def w_copy(k):
        return pltpu.make_async_copy(w_hbm.at[pl.ds(128 * k, 128)], raw.at[k], wl.at[k])

    ct_copy = pltpu.make_async_copy(ct_hbm, ct_ref, cl)
    for r in range(24):
        x_copy(r).start()
    for k in range(12):
        w_copy(k).start()
    ct_copy.start()
    x_t[...] = jnp.zeros_like(x_t)
    slope[:, tok:, :] = jnp.zeros((48, 256 - tok, 128), BF16)
    slope_next[:, tok:, :] = jnp.zeros((48, 256 - tok, 128), BF16)

    for r in range(24):
        x_copy(r).wait()
    x_move = pltpu.make_async_remote_copy(
        src_ref=x_row.at[pl.ds(12 - base, 12)], dst_ref=x_in, send_sem=xis, recv_sem=xir, device_id=x_dev, device_id_type=MESH)
    pl.semaphore_wait(barrier, 11)
    x_move.start()
    for k in range(12):
        w_copy(k).wait()
        for half in range(2):
            part[half] = raw[k, 64 * half:64 * half + 64].astype(F32).reshape(1536, 128)

            def sort_rows(r, _, k=k, half=half):
                w_ref[r * 12 + k, 64 * half:64 * half + 64, :] = part[half, pl.ds(r, 64, stride=24), :].astype(BF16)
                return 0

            lax.fori_loop(0, 24, sort_rows, 0, unroll=4)

    def pre_col(c):
        acc = None
        for gp in range(3):
            b0, b1 = meta_ref[96 * gp + c], meta_ref[96 * gp + 48 + c]
            r0, r1 = lax.div(b0, 12), lax.div(b1, 12)
            lhs = jnp.concatenate([x_row[r0], x_row[r1]], axis=1)
            rhs = jnp.concatenate([w_ref[b0], w_ref[b1]], axis=0)
            term = jnp.dot(lhs, rhs, preferred_element_type=F32)
            acc = term if acc is None else acc + term
        return acc

    q_a, q_b, q_c, q_d = (1 - yhi) * 2 + 1 - core, (1 - yhi) * 2 + core, yhi * 2 + 1 - core, t

    def piece(kind, src, dst, p, dev):
        return pltpu.make_async_remote_copy(
            src_ref=src, dst_ref=dst, send_sem=fs.at[kind, p], recv_sem=fr.at[kind, p], device_id=dev, device_id_type=MESH)

    def copy_a(p):
        return piece(0, s_a.at[pl.ds(COLS * p, COLS)], r_a.at[pl.ds(COLS * p, COLS)], p, core_dev)

    def copy_b(p):
        return piece(1, s_b.at[pl.ds(COLS * p, COLS)], r_b.at[pl.ds(COLS * p, COLS)], p, far_dev)

    def copy_c(p):
        return piece(2, s_c.at[pl.ds(COLS * p, COLS)], r_c.at[pl.ds(COLS * p, COLS)], p, core_dev)

    def slope_copy(kind, quarter, p, dev, src=0, dst=0):
        cols = pl.ds(quarter * 12 + COLS * p, COLS)
        held = {0: slope, 256: slope_next}
        return piece(kind, held[src].at[cols, pl.ds(0, tok)], held[dst].at[cols, pl.ds(0, tok)], p, dev)

    def far_copy(p):
        return slope_copy(3, q_d, p, far_dev)

    def core_copy(i, p):
        return slope_copy((4, 5, 8, 9)[i], q_b if i % 2 else q_d, p, core_dev, i // 2 * 256, i // 2 * 256)

    def x_copy_out(i, p):
        return slope_copy(6 + i, q_b if i else q_d, p, x_dev, 0, 256)

    def part_a(p, _):
        for i in [COLS * p + k for k in range(COLS)]:
            s_a[i] = pre_col(q_a * 12 + i).astype(BF16)
        copy_a(p).start()
        return 0

    def part_b(p, _):
        copy_a(p).wait_recv()
        for i in [COLS * p + k for k in range(COLS)]:
            s_b[i] = (pre_col(q_b * 12 + i) + r_a[i].astype(F32)).astype(BF16)
        copy_b(p).start()
        return 0

    def part_ab(p, _):
        part_a(p + 1, 0)
        return part_b(p, 0)

    def part_c(p, _):
        for i in [COLS * p + k for k in range(COLS)]:
            s_c[i] = pre_col(q_c * 12 + i).astype(BF16)
        copy_c(p).start()
        return 0

    def part_d(p, _):
        copy_c(p).wait_recv()
        for i in [COLS * p + k for k in range(COLS)]:
            part[p, pl.ds(tok * (i - COLS * p), tok), :] = pre_col(q_d * 12 + i) + r_c[i].astype(F32)
        return 0

    part_a(0, 0)
    lax.fori_loop(0, PIECES - 1, part_ab, 0)
    part_b(PIECES - 1, 0)
    lax.fori_loop(0, PIECES, part_c, 0)
    lax.fori_loop(0, PIECES, part_d, 0)

    def turn(r, _):
        x_t[r, :, 0:tok] = x_row[base + r].T
        x_t[r, :, 256:256 + tok] = x_in[r].T
        return 0

    def part_s(p, _):
        copy_b(p).wait_recv()
        for i in [COLS * p + k for k in range(COLS)]:
            pre = part[p, pl.ds(tok * (i - COLS * p), tok), :] + r_b[i].astype(F32)
            up = ct_ref[:, pl.ds(pl.multiple_of(i * 128, 128), 128)].astype(F32)
            slope[q_d * 12 + i, 0:tok, :] = (up * gelu_slope(pre)).astype(BF16)
        far_copy(p).start()
        core_copy(0, p).start()
        x_copy_out(0, p).start()
        return 0

    def turn_copy(p):
        return slope_copy(7, q_d, p, far_dev, 256, 256)

    def relay(p, _):
        slope_copy(6, q_d, p, x_dev, 256, 256).wait_recv()
        core_copy(2, p).start()
        slope_copy(3, q_b, p, far_dev).wait_recv()
        x_copy_out(1, p).start()
        core_copy(1, p).start()
        return 0

    def relay_far(p, _):
        slope_copy(6, q_d, p, x_dev, 256, 256).wait_recv()
        turn_copy(p).start()
        core_copy(2, p).start()
        return 0

    def relay_near(p, _):
        slope_copy(3, q_b, p, far_dev).wait_recv()
        core_copy(1, p).start()
        return 0

    def relay_last(p, _):
        slope_copy(7, q_b, p, x_dev, 256, 256).wait_recv()
        core_copy(3, p).start()
        return 0

    def gathered_own(p, _):
        slope_copy(4, q_c, p, core_dev).wait_recv()
        slope_copy(5, q_a, p, core_dev).wait_recv()
        return 0

    def gathered(p, _):
        slope_copy(8, q_c, p, core_dev, 256, 256).wait_recv()
        slope_copy(9, q_a, p, core_dev, 256, 256).wait_recv()
        return 0

    def column(r, slot):
        return meta_ref[288 + r * 12 + slot]

    def weight_part(j, first):
        xt = x_t[j, :, first:first + 256]
        slopes = slope_next if first else slope
        for kp in range(6):
            c0, c1 = column(base + j, 2 * kp), column(base + j, 2 * kp + 1)
            rhs = jnp.concatenate([slopes[c0], slopes[c1]], axis=1)
            g = jnp.dot(xt, rhs, preferred_element_type=F32)
            for half in range(2):
                rows = pl.ds(256 * kp + 128 * half, 128)
                v = g[:, 128 * half:128 * half + 128]
                part[j, rows, :] = v if first == 0 else part[j, rows, :] + v
        return 0

    def relay_and_own(p, _):
        for k in range(COLS):
            weight_part(COLS * p + k, 0)
        return relay_last(p, 0)

    def weight_rows(j, _):
        return weight_part(j, 256)

    ct_copy.wait()
    lax.fori_loop(0, PIECES, part_s, 0)
    x_move.wait_recv()
    lax.fori_loop(0, 12, turn, 0)
    lax.fori_loop(0, VIA_X, relay, 0)
    lax.fori_loop(VIA_X, PIECES, relay_far, 0)
    lax.fori_loop(VIA_X, PIECES, relay_near, 0)
    lax.fori_loop(0, PIECES, gathered_own, 0)
    lax.fori_loop(0, PIECES, relay_and_own, 0)
    lax.fori_loop(0, PIECES, gathered, 0)

    def input_rows(r, _):
        acc = None
        for kp in range(6):
            b = r * 12 + 2 * kp
            c0, c1 = column(r, 2 * kp), column(r, 2 * kp + 1)
            lhs = jnp.concatenate([slope[c0], slope[c1]], axis=1)[0:tok]
            rhs = jnp.concatenate([w_ref[b], w_ref[b + 1]], axis=1)
            term = lax.dot_general(lhs, rhs, (((1,), (1,)), ((), ())), preferred_element_type=F32)
            acc = term if acc is None else acc + term
        dx_ref[:, pl.ds(pl.multiple_of(r * 128, 128), 128)] = acc.astype(BF16)
        return 0

    z_units = [i for i, (g, _) in enumerate(UNITS) if GROUPS[g] in "zZ"]
    x_units = [i for i, (g, _) in enumerate(UNITS) if GROUPS[g] in "xX"]

    def half(unit):
        u = UNITS[unit][1]
        return ylo if u is None else u

    def load_z(unit, q, i):
        return part[ROWS * UNITS[unit][0] + i, pl.ds(pl.multiple_of(half(unit) * 768 + q * 96, 32), 96), :]

    def own_z(unit, i, v):
        two_z[z_units.index(unit), i] = v

    def load_x(unit, q, i):
        first = pl.multiple_of(half(unit) * 768 + q * 48, 16)
        row = ROWS * UNITS[unit][0] + i
        return jnp.concatenate([part[row, pl.ds(first + 96 * k, 48), :] for k in range(8)], axis=0)

    def own_x(unit, i, v):
        two_x[x_units.index(unit), i] = v.reshape(8, 48, 128)

    def load_u(unit, q, i):
        return two_x[x_units.index(unit), :, q].reshape(ROWS * 48, 128)

    def own_last(unit, i, v):
        done[x_units.index(unit)] = v.reshape(ROWS, 48, 128)

    stages = [
        {"z": Ring(8, z, zp, zm, z_units, load_z, own_z, z_send, z_recv, zss, zrs),
         "x": Ring(2, xhi, x_far, x_far, x_units, load_x, own_x, x_send, x_recv, xss, xrs)},
        {"x": Ring(8, z, zp, zm, x_units, load_u, own_last, u_send, u_recv, uss, urs)},
    ]

    firsts = [g for g, a in enumerate(GROUPS) if a.isupper()]

    def first_copy(g):
        i = firsts.index(g)
        return pltpu.make_async_remote_copy(
            src_ref=f_send.at[i], dst_ref=f_recv.at[i], send_sem=fss.at[i], recv_sem=frs.at[i], device_id=y_dev, device_id_type=MESH)

    def spread(g):
        unit = [i for i, u in enumerate(UNITS) if u[0] == g][0]
        in_z = unit in z_units
        sums = two_z if in_z else done
        index = (z_units if in_z else x_units).index(unit)
        for dx in range(4 if in_z else 2):
            for dy in range(1 if UNITS[unit][1] is None else 2):
                i = index if UNITS[unit][1] is None else index + lax.rem(ylo + dy, 2)
                q = lax.rem(x + dx, 4) if in_z else lax.rem(xlo + dx, 2)
                dev = (near if in_z else pair).get((dx, dy))
                yield dx, dy, dev, lambda i=i, q=q: sums[i, :, pl.ds(pl.multiple_of(24 * q, 8), 24), :]

    def give_copy(g, slot, dev):
        return pltpu.make_async_remote_copy(
            src_ref=g_send.at[g, slot], dst_ref=g_recv.at[g, slot], send_sem=gss.at[g, slot], recv_sem=grs.at[g, slot],
            device_id=dev, device_id_type=MESH)

    dx_copy = pltpu.make_async_copy(dx_ref, dx_hbm, dl)
    row = 0
    waits = []
    for kind, *what in ORDER:
        if kind == "D":
            lax.fori_loop(row, row + what[0], input_rows, 0)
            row += what[0]
            if row == 24:
                dx_copy.start()
            continue
        if kind in ("start", "step"):
            unit, stage = what[:2]
            ring = stages[stage - 1][GROUPS[UNITS[unit][0]].lower()]
            if kind == "start":
                ring.start(unit)
            else:
                ring.step(unit, what[2])
            continue
        g = what[0]
        unit = [i for i, u in enumerate(UNITS) if u[0] == g][0]
        if kind == "W":
            lax.fori_loop(ROWS * g, ROWS * g + ROWS, weight_rows, 0)
        elif kind == "y1s":
            def give(i, _, g=g):
                f_send[firsts.index(g), i] = part[ROWS * g + i, pl.ds(pl.multiple_of((1 - ylo) * 768, 768), 768), :].astype(BF16)
                return 0

            lax.fori_loop(0, ROWS, give, 0)
            first_copy(g).start()
            waits.append(first_copy(g))
        elif kind == "y1t":
            first_copy(g).wait_recv()

            def take(i, _, g=g):
                rows = pl.ds(pl.multiple_of(ylo * 768, 768), 768)
                part[ROWS * g + i, rows, :] = part[ROWS * g + i, rows, :] + f_recv[firsts.index(g), i].astype(F32)
                return 0

            lax.fori_loop(0, ROWS, take, 0)
        elif kind == "fs":
            for dx, dy, dev, value in spread(g):
                if dev is not None:
                    g_send[g, dx + 4 * dy] = value().reshape(ROWS * 24, 128).astype(BF16)
                    give_copy(g, dx + 4 * dy, dev).start()
                    waits.append(give_copy(g, dx + 4 * dy, dev))
        else:
            sums = [None, None]
            for dx, dy, dev, value in spread(g):
                if dev is None:
                    v = value().reshape(ROWS * 24, 128)
                else:
                    give_copy(g, dx + 4 * dy, dev).wait_recv()
                    v = g_recv[g, dx + 4 * dy].astype(F32)
                sums[dx % 2] = v if sums[dx % 2] is None else sums[dx % 2] + v
            for first, v in zip((base, 12 - base), sums):
                wg_rows[pl.ds(first + ROWS * g, ROWS)] = (v * scale).reshape(ROWS, 24, 128)
    assert row == 24
    for r in range(24):
        wg_ref[:, r, :] = wg_rows[r]

    def drain(p, _):
        copy_a(p).wait_send()
        copy_b(p).wait_send()
        copy_c(p).wait_send()
        far_copy(p).wait_send()
        for i in range(4):
            core_copy(i, p).wait_send()
        x_copy_out(0, p).wait_send()
        return 0

    def drain_x(p, _):
        x_copy_out(1, p).wait_send()
        return 0

    def drain_far(p, _):
        turn_copy(p).wait_send()
        return 0

    lax.fori_loop(0, PIECES, drain, 0)
    lax.fori_loop(0, VIA_X, drain_x, 0)
    lax.fori_loop(VIA_X, PIECES, drain_far, 0)
    x_move.wait_send()
    dx_copy.wait()
    for stage in stages:
        for ring in stage.values():
            ring.finish()
    for cp in waits:
        cp.wait_send()


def on_device(features, weights, block_cols, cotangent):
    tok, width = features.shape
    rows = weights.shape[1]
    row = jnp.arange(rows, dtype=jnp.int32)[:, None, None]
    slot = jnp.arange(12, dtype=jnp.int32)[None, :, None]
    place = jnp.arange(24 * rows, dtype=jnp.int32)[None, None, :]
    cols = block_cols[:, :, None]
    key = jnp.where(place < 12 * rows, row // 4 * 48 + cols, 12 * rows + row * 12 + slot)
    meta = jnp.sum(jnp.where(key == place, jnp.where(place < 12 * rows, row * 12 + slot, cols), 0), axis=(0, 1))
    scale = float(tok * lax.axis_size("dp")) ** (-0.5)
    vmem = pl.BlockSpec(memory_space=pltpu.VMEM)
    smem = pl.BlockSpec(memory_space=pltpu.SMEM)
    any_ = pl.BlockSpec(memory_space=pl.ANY)
    dma = pltpu.SemaphoreType.DMA
    quarter = pltpu.VMEM((12, tok, 128), BF16)
    n_groups = len(GROUPS)
    nz = sum(GROUPS[g] in "zZ" for g, _ in UNITS)
    nx = len(UNITS) - nz
    ny = max(1, sum(a.isupper() for a in GROUPS))
    dx, wg = pl.pallas_call(
        functools.partial(kernel, scale),
        out_shape=(jax.ShapeDtypeStruct((tok, width), BF16), jax.ShapeDtypeStruct((24, rows, 128), F32)),
        in_specs=[smem, any_, any_, any_],
        out_specs=(any_, vmem),
        scratch_shapes=[
            pltpu.VMEM((rows * 12, 128, 128), BF16),
            pltpu.VMEM((12, 128, rows, 128), BF16),
            pltpu.VMEM((tok, 1536), BF16),
            pltpu.VMEM((tok, width), BF16),
            quarter, quarter, quarter, quarter, quarter, quarter,
            pltpu.VMEM((48, 256, 128), BF16),
            pltpu.VMEM((48, 256, 128), BF16),
            pltpu.VMEM((rows, tok, 128), BF16),
            pltpu.VMEM((12, tok, 128), BF16),
            pltpu.VMEM((12, 128, 512), BF16),
            pltpu.VMEM((12, 1536, 128), F32),
            pltpu.VMEM((nz, ROWS, 96, 128), F32),
            pltpu.VMEM((nx, ROWS, 8, 48, 128), F32),
            pltpu.VMEM((nx, ROWS, 48, 128), F32),
            pltpu.VMEM((rows, 24, 128), F32),
            pltpu.VMEM((nz, 2, ROWS, 96, 128), BF16),
            pltpu.VMEM((nz, 7, ROWS, 96, 128), BF16),
            pltpu.VMEM((nx, 1, ROWS, 384, 128), BF16),
            pltpu.VMEM((nx, 1, ROWS, 384, 128), BF16),
            pltpu.VMEM((nx, 2, 1, ROWS * 48, 128), BF16),
            pltpu.VMEM((nx, 7, 1, ROWS * 48, 128), BF16),
            pltpu.VMEM((ny, ROWS, 768, 128), BF16),
            pltpu.VMEM((ny, ROWS, 768, 128), BF16),
            pltpu.VMEM((n_groups, 8, ROWS * 24, 128), BF16),
            pltpu.VMEM((n_groups, 8, ROWS * 24, 128), BF16),
            dma((rows,)), dma((12,)), dma(()), dma(()),
            dma((10, PIECES)), dma((10, PIECES)),
            dma(()), dma(()),
            dma((nz, 7)), dma((nz, 7)),
            dma((nx, 1)), dma((nx, 1)),
            dma((nx, 7)), dma((nx, 7)),
            dma((ny,)), dma((ny,)),
            dma((n_groups, 8)), dma((n_groups, 8)),
        ],
        compiler_params=pltpu.CompilerParams(
            collective_id=0, has_side_effects=True, vmem_limit_bytes=62 * 2**20),
        name="block_grads",
    )(meta, features, weights, cotangent)
    return dx, wg


def solution(mesh):
    return jax.shard_map(
        on_device,
        mesh=mesh,
        in_specs=(P("dp", "tensor"), P(None, "tensor", None), P("tensor", None), P("dp", "tensor")),
        out_specs=(P("dp", "tensor"), P("dp", "tensor", None)),
        check_vma=False,
    )
```

```python
import functools

import jax
import jax.numpy as jnp
from jax import lax
from jax.experimental import pallas as pl
from jax.experimental.pallas import tpu as pltpu
from jax.sharding import PartitionSpec as P

MESH = pl.DeviceIdType.MESH
F32 = jnp.float32
BF16 = jnp.bfloat16
gelu_coef = 0.7978845608

GROUPS = "zzxxXZ"
ROWS = 2
COLS = 3
PIECES = 12 // COLS
VIA_X = 3

ORDER = (
    ("W", 3), ("start", 7, 1), ("W", 4), ("y1s", 4), ("start", 6, 1), ("W", 0), ("start", 1, 1), ("start", 0, 1), ("W", 1), ("start", 3, 1),
    ("start", 2, 1), ("W", 2), ("start", 5, 1), ("W", 5), ("y1s", 5), ("step", 1, 1, 0), ("step", 7, 1, 0), ("start", 7, 2), ("D", 1),
    ("step", 0, 1, 0), ("D", 2), ("step", 3, 1, 0), ("D", 1), ("start", 4, 1), ("D", 1), ("step", 2, 1, 0), ("D", 3), ("step", 1, 1, 1), ("D", 1),
    ("step", 6, 1, 0), ("step", 7, 2, 0), ("start", 6, 2), ("D", 2), ("step", 0, 1, 1), ("y1t", 4), ("D", 1), ("start", 8, 1), ("D", 1),
    ("step", 3, 1, 1), ("D", 2), ("step", 2, 1, 1), ("D", 3), ("step", 5, 1, 0), ("step", 1, 1, 2), ("start", 5, 2), ("D", 1), ("step", 7, 2, 1),
    ("D", 1), ("step", 6, 2, 0), ("D", 2), ("step", 0, 1, 2), ("D", 2), ("step", 3, 1, 2), ("step", 4, 1, 0), ("start", 4, 2), ("step", 2, 1, 2),
    ("step", 1, 1, 3), ("y1t", 5), ("start", 9, 1), ("step", 5, 2, 0), ("step", 7, 2, 2), ("step", 6, 2, 1), ("step", 0, 1, 3), ("fs", 0),
    ("step", 3, 1, 3), ("step", 8, 1, 0), ("start", 8, 2), ("step", 4, 2, 0), ("step", 2, 1, 3), ("fs", 1), ("step", 9, 1, 0), ("step", 5, 2, 1),
    ("step", 7, 2, 3), ("step", 6, 2, 2), ("ft", 0), ("step", 8, 2, 0), ("step", 4, 2, 1), ("step", 9, 1, 1), ("ft", 1), ("step", 5, 2, 2),
    ("step", 6, 2, 3), ("fs", 3), ("step", 8, 2, 1), ("step", 4, 2, 2), ("step", 9, 1, 2), ("step", 5, 2, 3), ("step", 8, 2, 2), ("ft", 3),
    ("step", 4, 2, 3), ("fs", 2), ("step", 9, 1, 3), ("fs", 5), ("step", 8, 2, 3), ("fs", 4), ("ft", 2), ("ft", 5), ("ft", 4),
)

UNITS = [(g, u) for g, a in enumerate(GROUPS) for u in ((None,) if a.isupper() else (0, 1))]


def gelu_slope(v):
    th = jnp.tanh(gelu_coef * (v + 0.044715 * v * v * v))
    return 0.5 * (1.0 + th) + 0.5 * v * (1.0 - th * th) * gelu_coef * (1.0 + 0.134145 * v * v)


class Ring:
    def __init__(self, n, pos, ahead, back, units, load, own, send, recv, ssem, rsem):
        self.n, self.pos, self.devs, self.load, self.own = n, pos, (ahead, back), load, own
        self.send, self.recv, self.ssem, self.rsem = send, recv, ssem, rsem
        self.long = n // 2
        self.index = {unit: i for i, unit in enumerate(units)}
        self.started = []

    def ways(self, unit):
        g, u = UNITS[unit]
        first = (g if u is None else u) % 2
        return ((first, self.long, 0), (1 - first, self.n - 1 - self.long, self.long))

    def go(self, unit, way, slot, s):
        j = self.index[unit]
        src = self.send.at[j, way % self.send.shape[1]] if s == 0 else self.recv.at[j, slot + s - 1]
        cp = pltpu.make_async_remote_copy(
            src_ref=src, dst_ref=self.recv.at[j, slot + s], send_sem=self.ssem.at[j, slot + s], recv_sem=self.rsem.at[j, slot + s],
            device_id=self.devs[way], device_id_type=MESH)
        cp.start()
        self.started.append(cp)

    def arrived(self, unit, way, slot, s):
        j = self.index[unit]
        ref = self.recv.at[j, slot + s]
        pltpu.make_async_remote_copy(
            src_ref=ref, dst_ref=ref, send_sem=self.ssem.at[j, slot + s], recv_sem=self.rsem.at[j, slot + s],
            device_id=self.devs[way], device_id_type=MESH).wait_recv()

    def at(self, shift):
        return lax.rem(self.pos + (shift + 2 * self.n), self.n)

    def start(self, unit):
        j = self.index[unit]
        for way, far, slot in self.ways(unit):
            if far == 0:
                continue
            q = self.at(far if way == 0 else -far)

            def body(i, _, way=way, q=q):
                self.send[j, way % self.send.shape[1], i] = self.load(unit, q, i).astype(BF16)
                return 0

            lax.fori_loop(0, self.send.shape[2], body, 0)
            self.go(unit, way, slot, 0)

    def step(self, unit, s):
        j = self.index[unit]
        for way, far, slot in self.ways(unit):
            if s < far:
                self.arrived(unit, way, slot, s)
            if s < far - 1:
                q = self.at(far - 1 - s if way == 0 else 1 + s - far)

                def body(i, _, q=q, k=slot + s):
                    self.recv[j, k, i] = (self.recv[j, k, i].astype(F32) + self.load(unit, q, i)).astype(BF16)
                    return 0

                lax.fori_loop(0, self.send.shape[2], body, 0)
                self.go(unit, way, slot, s + 1)
        if s == self.long - 1:
            ends = [slot + far - 1 for _, far, slot in self.ways(unit) if far]

            def total(i, _):
                v = self.load(unit, self.pos, i)
                for k in ends:
                    v = v + self.recv[j, k, i].astype(F32)
                self.own(unit, i, v)
                return 0

            lax.fori_loop(0, self.send.shape[2], total, 0)

    def finish(self):
        for cp in self.started:
            cp.wait_send()


def kernel(scale, meta_ref, x_hbm, w_hbm, ct_hbm, dx_hbm, wg_ref,
           w_ref, raw, ct_ref, dx_ref, s_a, s_b, s_c, r_a, r_b, r_c, slope, slope_next, x_row, x_in, x_t, part, two_z, two_x, done, wg_rows,
           z_send, z_recv, x_send, x_recv, u_send, u_recv, f_send, f_recv, g_send, g_recv,
           xl, wl, cl, dl, fs, fr, xis, xir, zss, zrs, xss, xrs, uss, urs, fss, frs, gss, grs):
    d = lax.axis_index("dp")
    t = lax.axis_index("tensor")
    x, z, ylo = lax.rem(d, 4), lax.rem(d // 4, 8), d // 32
    yhi, core = t // 2, lax.rem(t, 2)

    def at(xx, zz, yy):
        return ((yy * 8 + zz) * 4 + xx, t)

    core_dev = (d, yhi * 2 + 1 - core)
    far_dev = (d, (1 - yhi) * 2 + core)
    y_dev = at(x, z, 1 - ylo)
    zp, zm = at(x, lax.rem(z + 1, 8), ylo), at(x, lax.rem(z + 7, 8), ylo)
    xhi, xlo = x // 2, lax.rem(x, 2)
    near = {(dx, dy): at(lax.rem(x + dx, 4), z, lax.rem(ylo + dy, 2)) for dx in range(4) for dy in range(2) if dx or dy}
    x_far, x_dev = near[2, 0], at(x + 1 - 2 * xlo, z, ylo)
    pair = {(0, 1): y_dev, (1, 0): x_dev, (1, 1): at(x + 1 - 2 * xlo, z, 1 - ylo)}
    base = 12 * xlo

    barrier = pltpu.get_barrier_semaphore()
    for dev in (core_dev, far_dev, zp, zm, *near.values()):
        pl.semaphore_signal(barrier, inc=1, device_id=dev, device_id_type=MESH)

    tok = x_hbm.shape[0]

    def x_copy(r):
        return pltpu.make_async_copy(x_hbm.at[:, pl.ds(128 * r, 128)], x_row.at[r], xl.at[r])

    def w_copy(k):
        return pltpu.make_async_copy(w_hbm.at[pl.ds(128 * k, 128)], raw.at[k], wl.at[k])

    ct_copy = pltpu.make_async_copy(ct_hbm, ct_ref, cl)
    for r in range(24):
        x_copy(r).start()
    for k in range(12):
        w_copy(k).start()
    ct_copy.start()
    x_t[...] = jnp.zeros_like(x_t)
    slope[:, tok:, :] = jnp.zeros((48, 256 - tok, 128), BF16)
    slope_next[:, tok:, :] = jnp.zeros((48, 256 - tok, 128), BF16)

    for r in range(24):
        x_copy(r).wait()
    x_move = pltpu.make_async_remote_copy(
        src_ref=x_row.at[pl.ds(12 - base, 12)], dst_ref=x_in, send_sem=xis, recv_sem=xir, device_id=x_dev, device_id_type=MESH)
    pl.semaphore_wait(barrier, 11)
    x_move.start()
    for k in range(12):
        w_copy(k).wait()
        for half in range(2):
            part[half] = raw[k, 64 * half:64 * half + 64].astype(F32).reshape(1536, 128)

            def sort_rows(r, _, k=k, half=half):
                w_ref[r * 12 + k, 64 * half:64 * half + 64, :] = part[half, pl.ds(r, 64, stride=24), :].astype(BF16)
                return 0

            lax.fori_loop(0, 24, sort_rows, 0, unroll=4)

    def pre_col(c):
        acc = None
        for gp in range(3):
            b0, b1 = meta_ref[96 * gp + c], meta_ref[96 * gp + 48 + c]
            r0, r1 = lax.div(b0, 12), lax.div(b1, 12)
            lhs = jnp.concatenate([x_row[r0], x_row[r1]], axis=1)
            rhs = jnp.concatenate([w_ref[b0], w_ref[b1]], axis=0)
            term = jnp.dot(lhs, rhs, preferred_element_type=F32)
            acc = term if acc is None else acc + term
        return acc

    q_a, q_b, q_c, q_d = (1 - yhi) * 2 + 1 - core, (1 - yhi) * 2 + core, yhi * 2 + 1 - core, t

    def piece(kind, src, dst, p, dev):
        return pltpu.make_async_remote_copy(
            src_ref=src, dst_ref=dst, send_sem=fs.at[kind, p], recv_sem=fr.at[kind, p], device_id=dev, device_id_type=MESH)

    def copy_a(p):
        return piece(0, s_a.at[pl.ds(COLS * p, COLS)], r_a.at[pl.ds(COLS * p, COLS)], p, core_dev)

    def copy_b(p):
        return piece(1, s_b.at[pl.ds(COLS * p, COLS)], r_b.at[pl.ds(COLS * p, COLS)], p, far_dev)

    def copy_c(p):
        return piece(2, s_c.at[pl.ds(COLS * p, COLS)], r_c.at[pl.ds(COLS * p, COLS)], p, core_dev)

    def slope_copy(kind, quarter, p, dev, src=0, dst=0):
        cols = pl.ds(quarter * 12 + COLS * p, COLS)
        held = {0: slope, 256: slope_next}
        return piece(kind, held[src].at[cols, pl.ds(0, tok)], held[dst].at[cols, pl.ds(0, tok)], p, dev)

    def far_copy(p):
        return slope_copy(3, q_d, p, far_dev)

    def core_copy(i, p):
        return slope_copy((4, 5, 8, 9)[i], q_b if i % 2 else q_d, p, core_dev, i // 2 * 256, i // 2 * 256)

    def x_copy_out(i, p):
        return slope_copy(6 + i, q_b if i else q_d, p, x_dev, 0, 256)

    def part_a(p, _):
        for i in [COLS * p + k for k in range(COLS)]:
            s_a[i] = pre_col(q_a * 12 + i).astype(BF16)
        copy_a(p).start()
        return 0

    def part_b(p, _):
        copy_a(p).wait_recv()
        for i in [COLS * p + k for k in range(COLS)]:
            s_b[i] = (pre_col(q_b * 12 + i) + r_a[i].astype(F32)).astype(BF16)
        copy_b(p).start()
        return 0

    def part_ab(p, _):
        part_a(p + 1, 0)
        return part_b(p, 0)

    def part_c(p, _):
        for i in [COLS * p + k for k in range(COLS)]:
            s_c[i] = pre_col(q_c * 12 + i).astype(BF16)
        copy_c(p).start()
        return 0

    def part_d(p, _):
        copy_c(p).wait_recv()
        for i in [COLS * p + k for k in range(COLS)]:
            part[p, pl.ds(tok * (i - COLS * p), tok), :] = pre_col(q_d * 12 + i) + r_c[i].astype(F32)
        return 0

    part_a(0, 0)
    lax.fori_loop(0, PIECES - 1, part_ab, 0)
    part_b(PIECES - 1, 0)
    lax.fori_loop(0, PIECES, part_c, 0)
    lax.fori_loop(0, PIECES, part_d, 0)

    def turn(r, _):
        x_t[r, :, 0:tok] = x_row[base + r].T
        x_t[r, :, 256:256 + tok] = x_in[r].T
        return 0

    def part_s(p, _):
        copy_b(p).wait_recv()
        for i in [COLS * p + k for k in range(COLS)]:
            pre = part[p, pl.ds(tok * (i - COLS * p), tok), :] + r_b[i].astype(F32)
            up = ct_ref[:, pl.ds(pl.multiple_of(i * 128, 128), 128)].astype(F32)
            slope[q_d * 12 + i, 0:tok, :] = (up * gelu_slope(pre)).astype(BF16)
        far_copy(p).start()
        core_copy(0, p).start()
        x_copy_out(0, p).start()
        return 0

    def turn_copy(p):
        return slope_copy(7, q_d, p, far_dev, 256, 256)

    def relay(p, _):
        slope_copy(6, q_d, p, x_dev, 256, 256).wait_recv()
        core_copy(2, p).start()
        slope_copy(3, q_b, p, far_dev).wait_recv()
        x_copy_out(1, p).start()
        core_copy(1, p).start()
        return 0

    def relay_far(p, _):
        slope_copy(6, q_d, p, x_dev, 256, 256).wait_recv()
        turn_copy(p).start()
        core_copy(2, p).start()
        return 0

    def relay_near(p, _):
        slope_copy(3, q_b, p, far_dev).wait_recv()
        core_copy(1, p).start()
        return 0

    def relay_last(p, _):
        slope_copy(7, q_b, p, x_dev, 256, 256).wait_recv()
        core_copy(3, p).start()
        return 0

    def gathered_own(p, _):
        slope_copy(4, q_c, p, core_dev).wait_recv()
        slope_copy(5, q_a, p, core_dev).wait_recv()
        return 0

    def gathered(p, _):
        slope_copy(8, q_c, p, core_dev, 256, 256).wait_recv()
        slope_copy(9, q_a, p, core_dev, 256, 256).wait_recv()
        return 0

    def column(r, slot):
        return meta_ref[288 + r * 12 + slot]

    def weight_part(j, first):
        xt = x_t[j, :, first:first + 256]
        slopes = slope_next if first else slope
        for kp in range(6):
            c0, c1 = column(base + j, 2 * kp), column(base + j, 2 * kp + 1)
            rhs = jnp.concatenate([slopes[c0], slopes[c1]], axis=1)
            g = jnp.dot(xt, rhs, preferred_element_type=F32)
            for half in range(2):
                rows = pl.ds(256 * kp + 128 * half, 128)
                v = g[:, 128 * half:128 * half + 128]
                part[j, rows, :] = v if first == 0 else part[j, rows, :] + v
        return 0

    def relay_and_own(p, _):
        for k in range(COLS):
            weight_part(COLS * p + k, 0)
        return relay_last(p, 0)

    def weight_rows(j, _):
        return weight_part(j, 256)

    ct_copy.wait()
    lax.fori_loop(0, PIECES, part_s, 0)
    x_move.wait_recv()
    lax.fori_loop(0, 12, turn, 0)
    lax.fori_loop(0, VIA_X, relay, 0)
    lax.fori_loop(VIA_X, PIECES, relay_far, 0)
    lax.fori_loop(VIA_X, PIECES, relay_near, 0)
    lax.fori_loop(0, PIECES, gathered_own, 0)
    lax.fori_loop(0, PIECES, relay_and_own, 0)
    lax.fori_loop(0, PIECES, gathered, 0)

    def input_rows(r, _):
        acc = None
        for kp in range(6):
            b = r * 12 + 2 * kp
            c0, c1 = column(r, 2 * kp), column(r, 2 * kp + 1)
            lhs = jnp.concatenate([slope[c0], slope[c1]], axis=1)[0:tok]
            rhs = jnp.concatenate([w_ref[b], w_ref[b + 1]], axis=1)
            term = lax.dot_general(lhs, rhs, (((1,), (1,)), ((), ())), preferred_element_type=F32)
            acc = term if acc is None else acc + term
        dx_ref[:, pl.ds(pl.multiple_of(r * 128, 128), 128)] = acc.astype(BF16)
        return 0

    z_units = [i for i, (g, _) in enumerate(UNITS) if GROUPS[g] in "zZ"]
    x_units = [i for i, (g, _) in enumerate(UNITS) if GROUPS[g] in "xX"]

    def half(unit):
        u = UNITS[unit][1]
        return ylo if u is None else u

    def load_z(unit, q, i):
        return part[ROWS * UNITS[unit][0] + i, pl.ds(pl.multiple_of(half(unit) * 768 + q * 96, 32), 96), :]

    def own_z(unit, i, v):
        two_z[z_units.index(unit), i] = v

    def load_x(unit, q, i):
        first = pl.multiple_of(half(unit) * 768 + q * 48, 16)
        row = ROWS * UNITS[unit][0] + i
        return jnp.concatenate([part[row, pl.ds(first + 96 * k, 48), :] for k in range(8)], axis=0)

    def own_x(unit, i, v):
        two_x[x_units.index(unit), i] = v.reshape(8, 48, 128)

    def load_u(unit, q, i):
        return two_x[x_units.index(unit), :, q].reshape(ROWS * 48, 128)

    def own_last(unit, i, v):
        done[x_units.index(unit)] = v.reshape(ROWS, 48, 128)

    stages = [
        {"z": Ring(8, z, zp, zm, z_units, load_z, own_z, z_send, z_recv, zss, zrs),
         "x": Ring(2, xhi, x_far, x_far, x_units, load_x, own_x, x_send, x_recv, xss, xrs)},
        {"x": Ring(8, z, zp, zm, x_units, load_u, own_last, u_send, u_recv, uss, urs)},
    ]

    firsts = [g for g, a in enumerate(GROUPS) if a.isupper()]

    def first_copy(g):
        i = firsts.index(g)
        return pltpu.make_async_remote_copy(
            src_ref=f_send.at[i], dst_ref=f_recv.at[i], send_sem=fss.at[i], recv_sem=frs.at[i], device_id=y_dev, device_id_type=MESH)

    def spread(g):
        unit = [i for i, u in enumerate(UNITS) if u[0] == g][0]
        in_z = unit in z_units
        sums = two_z if in_z else done
        index = (z_units if in_z else x_units).index(unit)
        for dx in range(4 if in_z else 2):
            for dy in range(1 if UNITS[unit][1] is None else 2):
                i = index if UNITS[unit][1] is None else index + lax.rem(ylo + dy, 2)
                q = lax.rem(x + dx, 4) if in_z else lax.rem(xlo + dx, 2)
                dev = (near if in_z else pair).get((dx, dy))
                yield dx, dy, dev, lambda i=i, q=q: sums[i, :, pl.ds(pl.multiple_of(24 * q, 8), 24), :]

    def give_copy(g, slot, dev):
        return pltpu.make_async_remote_copy(
            src_ref=g_send.at[g, slot], dst_ref=g_recv.at[g, slot], send_sem=gss.at[g, slot], recv_sem=grs.at[g, slot],
            device_id=dev, device_id_type=MESH)

    dx_copy = pltpu.make_async_copy(dx_ref, dx_hbm, dl)
    row = 0
    waits = []
    for kind, *what in ORDER:
        if kind == "D":
            lax.fori_loop(row, row + what[0], input_rows, 0)
            row += what[0]
            if row == 24:
                dx_copy.start()
            continue
        if kind in ("start", "step"):
            unit, stage = what[:2]
            ring = stages[stage - 1][GROUPS[UNITS[unit][0]].lower()]
            if kind == "start":
                ring.start(unit)
            else:
                ring.step(unit, what[2])
            continue
        g = what[0]
        unit = [i for i, u in enumerate(UNITS) if u[0] == g][0]
        if kind == "W":
            lax.fori_loop(ROWS * g, ROWS * g + ROWS, weight_rows, 0)
        elif kind == "y1s":
            def give(i, _, g=g):
                f_send[firsts.index(g), i] = part[ROWS * g + i, pl.ds(pl.multiple_of((1 - ylo) * 768, 768), 768), :].astype(BF16)
                return 0

            lax.fori_loop(0, ROWS, give, 0)
            first_copy(g).start()
            waits.append(first_copy(g))
        elif kind == "y1t":
            first_copy(g).wait_recv()

            def take(i, _, g=g):
                rows = pl.ds(pl.multiple_of(ylo * 768, 768), 768)
                part[ROWS * g + i, rows, :] = part[ROWS * g + i, rows, :] + f_recv[firsts.index(g), i].astype(F32)
                return 0

            lax.fori_loop(0, ROWS, take, 0)
        elif kind == "fs":
            for dx, dy, dev, value in spread(g):
                if dev is not None:
                    g_send[g, dx + 4 * dy] = value().reshape(ROWS * 24, 128).astype(BF16)
                    give_copy(g, dx + 4 * dy, dev).start()
                    waits.append(give_copy(g, dx + 4 * dy, dev))
        else:
            sums = [None, None]
            for dx, dy, dev, value in spread(g):
                if dev is None:
                    v = value().reshape(ROWS * 24, 128)
                else:
                    give_copy(g, dx + 4 * dy, dev).wait_recv()
                    v = g_recv[g, dx + 4 * dy].astype(F32)
                sums[dx % 2] = v if sums[dx % 2] is None else sums[dx % 2] + v
            for first, v in zip((base, 12 - base), sums):
                wg_rows[pl.ds(first + ROWS * g, ROWS)] = (v * scale).reshape(ROWS, 24, 128)
    assert row == 24
    for r in range(24):
        wg_ref[:, r, :] = wg_rows[r]

    def drain(p, _):
        copy_a(p).wait_send()
        copy_b(p).wait_send()
        copy_c(p).wait_send()
        far_copy(p).wait_send()
        for i in range(4):
            core_copy(i, p).wait_send()
        x_copy_out(0, p).wait_send()
        return 0

    def drain_x(p, _):
        x_copy_out(1, p).wait_send()
        return 0

    def drain_far(p, _):
        turn_copy(p).wait_send()
        return 0

    lax.fori_loop(0, PIECES, drain, 0)
    lax.fori_loop(0, VIA_X, drain_x, 0)
    lax.fori_loop(VIA_X, PIECES, drain_far, 0)
    x_move.wait_send()
    dx_copy.wait()
    for stage in stages:
        for ring in stage.values():
            ring.finish()
    for cp in waits:
        cp.wait_send()


def hand_on(dx_ref, wg_ref, dx_out, wg_out):
    dx_out[...] = dx_ref[...]
    wg_out[...] = wg_ref[...]


def on_device(features, weights, block_cols, cotangent):
    tok, width = features.shape
    rows = weights.shape[1]
    row = jnp.arange(rows, dtype=jnp.int32)[:, None, None]
    slot = jnp.arange(12, dtype=jnp.int32)[None, :, None]
    place = jnp.arange(24 * rows, dtype=jnp.int32)[None, None, :]
    cols = block_cols[:, :, None]
    key = jnp.where(place < 12 * rows, row // 4 * 48 + cols, 12 * rows + row * 12 + slot)
    meta = jnp.sum(jnp.where(key == place, jnp.where(place < 12 * rows, row * 12 + slot, cols), 0), axis=(0, 1))
    scale = float(tok * lax.axis_size("dp")) ** (-0.5)
    vmem = pl.BlockSpec(memory_space=pltpu.VMEM)
    smem = pl.BlockSpec(memory_space=pltpu.SMEM)
    any_ = pl.BlockSpec(memory_space=pl.ANY)
    dma = pltpu.SemaphoreType.DMA
    quarter = pltpu.VMEM((12, tok, 128), BF16)
    n_groups = len(GROUPS)
    nz = sum(GROUPS[g] in "zZ" for g, _ in UNITS)
    nx = len(UNITS) - nz
    ny = max(1, sum(a.isupper() for a in GROUPS))
    dx, wg = pl.pallas_call(
        functools.partial(kernel, scale),
        out_shape=(jax.ShapeDtypeStruct((tok, width), BF16), jax.ShapeDtypeStruct((24, rows, 128), F32)),
        in_specs=[smem, any_, any_, any_],
        out_specs=(any_, vmem),
        scratch_shapes=[
            pltpu.VMEM((rows * 12, 128, 128), BF16),
            pltpu.VMEM((12, 128, rows, 128), BF16),
            pltpu.VMEM((tok, 1536), BF16),
            pltpu.VMEM((tok, width), BF16),
            quarter, quarter, quarter, quarter, quarter, quarter,
            pltpu.VMEM((48, 256, 128), BF16),
            pltpu.VMEM((48, 256, 128), BF16),
            pltpu.VMEM((rows, tok, 128), BF16),
            pltpu.VMEM((12, tok, 128), BF16),
            pltpu.VMEM((12, 128, 512), BF16),
            pltpu.VMEM((12, 1536, 128), F32),
            pltpu.VMEM((nz, ROWS, 96, 128), F32),
            pltpu.VMEM((nx, ROWS, 8, 48, 128), F32),
            pltpu.VMEM((nx, ROWS, 48, 128), F32),
            pltpu.VMEM((rows, 24, 128), F32),
            pltpu.VMEM((nz, 2, ROWS, 96, 128), BF16),
            pltpu.VMEM((nz, 7, ROWS, 96, 128), BF16),
            pltpu.VMEM((nx, 1, ROWS, 384, 128), BF16),
            pltpu.VMEM((nx, 1, ROWS, 384, 128), BF16),
            pltpu.VMEM((nx, 2, 1, ROWS * 48, 128), BF16),
            pltpu.VMEM((nx, 7, 1, ROWS * 48, 128), BF16),
            pltpu.VMEM((ny, ROWS, 768, 128), BF16),
            pltpu.VMEM((ny, ROWS, 768, 128), BF16),
            pltpu.VMEM((n_groups, 8, ROWS * 24, 128), BF16),
            pltpu.VMEM((n_groups, 8, ROWS * 24, 128), BF16),
            dma((rows,)), dma((12,)), dma(()), dma(()),
            dma((10, PIECES)), dma((10, PIECES)),
            dma(()), dma(()),
            dma((nz, 7)), dma((nz, 7)),
            dma((nx, 1)), dma((nx, 1)),
            dma((nx, 7)), dma((nx, 7)),
            dma((ny,)), dma((ny,)),
            dma((n_groups, 8)), dma((n_groups, 8)),
        ],
        compiler_params=pltpu.CompilerParams(
            collective_id=0, has_side_effects=True, vmem_limit_bytes=62 * 2**20),
        name="block_grads",
    )(meta, features, weights, cotangent)
    return pl.pallas_call(
        hand_on,
        out_shape=(jax.ShapeDtypeStruct((tok, width), BF16), jax.ShapeDtypeStruct((24, rows, 128), F32)),
        in_specs=[vmem, vmem],
        out_specs=(vmem, vmem),

        name="hand_on",
    )(dx, wg)


def solution(mesh):
    return jax.shard_map(
        on_device,
        mesh=mesh,
        in_specs=(P("dp", "tensor"), P(None, "tensor", None), P("tensor", None), P("dp", "tensor")),
        out_specs=(P("dp", "tensor"), P("dp", "tensor", None)),
        check_vma=False,
    )
```
